256 devices in a mesh: tm: 32 (over z, x), dp: 8 (over y, core).
Axes of the slice: x: 4, y: 4, z: 8, core: 2. Of those that a mesh axis runs over, the one named last changes fastest.
Arguments:
- frames: bfloat16 [8, 4096, 1024], P('dp', 'tm'), may hold values from -6 to 6
- grad_frames: bfloat16 [8, 4096, 1024], P('dp', 'tm'), may hold values from -6 to 6
- w_qkv: bfloat16 [1024, 2304], replicated, may hold values from -0.1875 to 0.1875
- w_out: bfloat16 [1024, 768], replicated, may hold values from -0.21875 to 0.21875
Outputs:
- grad_input: bfloat16 [8, 4096, 1024], P('dp', 'tm')
- grad_qkv: float32 [1024, 2304], P('tm')
- grad_out: float32 [1024, 768], P('tm')
The draws below stay inside these ranges and needn't reach their ends.
All inputs are finite; a program needn't handle non-finite values.
Results may differ from the reference program's by a relative error of at most 0.014.
Values sent between devices are 32-bit elements; how exact they have to be, the bound alone decides.
No kernel may reach another device: no remote copies, remote signals or barrier semaphores. Data moves between devices by JAX's collectives and lax.ppermute only.
A program may use at most 64 MiB of HBM per device.

```python
import jax
import jax.numpy as jnp
from jax import lax

D = 1024
HEADS = 12
HEAD = 64
HE = 768
BLOCK = 128
LEN = 4096
UTTS = 8


def raised(drawn, rng, source, target, shards_of, factor):
    def block_of(position):
        return (jnp.arange(drawn.shape[position]) // (drawn.shape[position] // shards_of)).reshape((-1,) + (1,) * (drawn.ndim - 1 - position))

    first = jax.random.permutation(rng, shards_of)[block_of(target)]
    other_side = (block_of(target) + shards_of // 2) % shards_of
    return jnp.where((block_of(source) == first) | (block_of(source) == other_side), factor * drawn, drawn)


def shard_levels(own_key, extent, shards, smallest, top_value):
    def one(position, blocks):
        draws = jax.random.uniform(jax.random.fold_in(jax.random.fold_in(own_key, 6), position), (blocks,), jnp.float32, smallest / len(shards), top_value / len(shards))
        return jnp.repeat(jnp.exp(draws), extent[position] // blocks).reshape((-1,) + (1,) * (len(extent) - position - 1))

    level = one(*shards[0])
    for cut in shards[1:]:
        level = level * one(*cut)
    return level


def gaussian(rng, dims, scale, limit, split=(), held_as=jnp.bfloat16):
    factor_of = shard_levels(rng, dims, split, -0.22, 0.18) if split else 1.0
    array = jax.random.normal(rng, dims, jnp.float32) * scale * factor_of
    return jnp.minimum(jnp.maximum(array, -limit), limit).astype(held_as)


def gaussian_with(key, shape, spread, reach, pieces, heavy, kind=jnp.bfloat16):
    drawn = spread * jax.random.normal(key, shape, jnp.float32)
    if pieces:
        drawn = drawn * shard_levels(key, shape, pieces, -0.22, 0.18)
    return jnp.clip(raised(drawn, jax.random.fold_in(key, 3), *heavy), -reach, reach).astype(kind)


def setup_inputs(seed: int = 0) -> dict:
    seeds = jax.random.split(jax.random.key(seed), 5)
    return {
        "frames": gaussian_with(seeds[0], (UTTS, LEN, D), 1.0, 6.0, ((0, 8), (1, 32)), (1, 2, 32, 2.75)),
        "grad_frames": gaussian_with(seeds[1], (UTTS, LEN, D), 1.0, 6.0, ((0, 8), (1, 32)), (1, 2, 32, 2.75)),
        "w_qkv": gaussian(seeds[2], (D, 3 * HE), D ** -0.5, 0.1875),
        "w_out": gaussian(seeds[3], (D, HE), HE ** -0.5, 0.21875),
    }


def features(a):
    return jnp.where(a > 0, a + 1.0, jnp.exp(jnp.minimum(a, 0.0)))


def slope(a):
    return jnp.where(a > 0, 1.0, jnp.exp(jnp.minimum(a, 0.0)))


def one_utterance(x, dy, w_qkv, w_out):
    f32 = jnp.float32
    bf = jnp.bfloat16
    qkv = jnp.dot(x, w_qkv, preferred_element_type=f32).astype(bf)
    q = qkv[:, :HE].astype(f32)
    k = qkv[:, HE:2 * HE].astype(f32)
    fq = features(q).astype(bf)
    fk = features(k).astype(bf)
    v = qkv[:, 2 * HE:]
    g = jnp.dot(dy, w_out, preferred_element_type=f32).astype(bf)
    nblk = x.shape[0] // BLOCK
    shape4 = (nblk, BLOCK, HEADS, HEAD)
    fqb, fkb, vb, gb = fq.reshape(shape4), fk.reshape(shape4), v.reshape(shape4), g.reshape(shape4)
    mask = jnp.tril(jnp.ones((BLOCK, BLOCK), bool))

    def forward(carry, item_list):
        running_state, running_norm = carry
        query_feature_map, key_feature_map, value_rows, output_gradient_rows = item_list
        fq32, fk32, v32, g32 = query_feature_map.astype(f32), key_feature_map.astype(f32), value_rows.astype(f32), output_gradient_rows.astype(f32)
        block_state = running_state.astype(bf)
        scores = jnp.where(mask, jnp.einsum('thd,shd->hts', fq32, fk32), 0.0)
        den = scores.sum(-1).T + jnp.sum(fq32 * running_norm[None], -1)
        weights = scores.astype(bf).astype(f32)
        num = jnp.einsum('hts,she->the', weights, v32) + jnp.einsum('thd,hde->the', fq32, block_state.astype(f32))
        ratio = num / den[..., None]
        attention_block = ratio.astype(bf)
        numerator_gradient = (g32 / den[..., None]).astype(bf)
        denominator_gradient = -jnp.sum(g32 * ratio, -1) / den
        block_score_gradient = jnp.einsum('thd,the->hde', fq32, numerator_gradient.astype(f32))
        block_normalizer_gradient = jnp.sum(denominator_gradient[..., None] * fq32, 0)
        new = (running_state + jnp.einsum('shd,she->hde', fk32, v32), running_norm + jnp.sum(fk32, 0))
        return new, (attention_block, block_state, running_norm, numerator_gradient, denominator_gradient, block_score_gradient, block_normalizer_gradient)

    init = (jnp.zeros((HEADS, HEAD, HEAD), f32), jnp.zeros((HEADS, HEAD), f32))
    _, outs = lax.scan(forward, init, (fqb, fkb, vb, gb))
    attention_block, block_state, running_norm, numerator_gradient, denominator_gradient, block_score_gradient, block_normalizer_gradient = outs

    def backward(carry, item_list):
        dstate, dnorm = carry
        query_feature_map, key_feature_map, value_rows, sb, nz, dn, dd, dsb, dzb = item_list
        fq32, fk32, v32, dn32 = query_feature_map.astype(f32), key_feature_map.astype(f32), value_rows.astype(f32), dn.astype(f32)
        dstate_b = dstate.astype(bf).astype(f32)
        sb32 = sb.astype(f32)
        scores = jnp.where(mask, jnp.einsum('thd,shd->hts', fq32, fk32), 0.0)
        weights = scores.astype(bf).astype(f32)
        dscore = jnp.einsum('the,she->hts', dn32, v32) + dd.T[:, :, None]
        dscore = jnp.where(mask, dscore, 0.0).astype(bf).astype(f32)
        dfq = jnp.einsum('hts,shd->thd', dscore, fk32) + jnp.einsum('the,hde->thd', dn32, sb32) + dd[..., None] * nz[None]
        dfk = jnp.einsum('hts,thd->shd', dscore, fq32) + jnp.einsum('she,hde->shd', v32, dstate_b) + dnorm[None]
        dv = jnp.einsum('hts,the->she', weights, dn32) + jnp.einsum('shd,hde->she', fk32, dstate_b)
        return (dstate + dsb, dnorm + dzb), (dfq, dfk, dv)

    _, grads = lax.scan(backward, init, (fqb, fkb, vb, block_state, running_norm, numerator_gradient, denominator_gradient, block_score_gradient, block_normalizer_gradient), reverse=True)
    dfq, dfk, dv = grads
    rows = x.shape[0]
    dq = dfq.reshape(rows, HE) * slope(q)
    dk = dfk.reshape(rows, HE) * slope(k)
    dqkv = jnp.concatenate([dq, dk, dv.reshape(rows, HE)], axis=1).astype(bf)
    dx = jnp.dot(dqkv, w_qkv.T, preferred_element_type=f32).astype(bf)
    attention_block = attention_block.reshape(rows, HE)
    gq = jnp.dot(x.T, dqkv, preferred_element_type=f32)
    go = jnp.dot(dy.T, attention_block, preferred_element_type=f32)
    return dx, gq, go


def reference(frames, grad_frames, w_qkv, w_out):
    dx, gq, go = lax.map(lambda pair: one_utterance(pair[0], pair[1], w_qkv, w_out), (frames, grad_frames))
    return dx, jnp.sum(gq, 0), jnp.sum(go, 0)
```

```python
import functools

import jax
import jax.numpy as jnp
from jax import lax
from jax.experimental import pallas as pl
from jax.experimental.pallas import tpu as pltpu
from jax.sharding import Mesh
from jax.sharding import PartitionSpec as P

HEADS = 12
HEAD = 64
BLOCK = 128
PAIRS = HEADS // 2
INNER = HEADS * HEAD
TM = ("z", "x")
DP = ("y", "c")
F32 = jnp.float32
BF16 = jnp.bfloat16
VMEM_LIMIT = 40 * 1024 * 1024


def features(a):
    return jnp.where(a > 0, a + 1.0, jnp.exp(jnp.minimum(a, 0.0)))


def slope(a):
    return jnp.where(a > 0, 1.0, jnp.exp(jnp.minimum(a, 0.0)))


def low_lanes(shape):
    return lax.broadcasted_iota(jnp.int32, shape, len(shape) - 1) < HEAD


def split_pair(a):
    low = low_lanes(a.shape)
    zero = jnp.zeros_like(a)
    return jnp.where(low, a, zero), jnp.where(low, zero, a)


def block_diagonal(packed):
    first, second = split_pair(packed)
    return jnp.concatenate([first, second], axis=0)


def diagonal_blocks(m):
    return jnp.where(low_lanes((HEAD, 2 * HEAD)), m[:HEAD], m[HEAD:])


def mm(a, b):
    return lax.dot_general(a, b, (((1,), (0,)), ((), ())), preferred_element_type=F32)


def mm_bt(a, b):
    return lax.dot_general(a, b, (((1,), (1,)), ((), ())), preferred_element_type=F32)


def mm_at(a, b):
    return lax.dot_general(a, b, (((0,), (0,)), ((), ())), preferred_element_type=F32)


def causal():
    rows = lax.broadcasted_iota(jnp.int32, (BLOCK, BLOCK), 0)
    columns = lax.broadcasted_iota(jnp.int32, (BLOCK, BLOCK), 1)
    return columns <= rows


def project_kernel(x_ref, dy_ref, wq_ref, wk_ref, wv_ref, wo_ref, q_ref, k_ref, v_ref, g_ref, send_ref):
    step = pl.program_id(0)

    @pl.when(step == 0)
    def _():
        send_ref[...] = jnp.zeros_like(send_ref)

    x = x_ref[...]
    q_ref[...] = mm(x, wq_ref[...]).astype(BF16)
    k = mm(x, wk_ref[...]).astype(BF16)
    k_ref[...] = k
    v = mm(x, wv_ref[...]).astype(BF16)
    v_ref[...] = v
    g_ref[...] = mm(dy_ref[...], wo_ref[...]).astype(BF16)
    fk = features(k.astype(F32)).astype(BF16)
    for i in range(2):
        lanes = slice(128 * i, 128 * i + 128)
        state = diagonal_blocks(mm_at(fk[:, lanes], v[:, lanes]))
        norm = jnp.sum(fk[:, lanes].astype(F32), axis=0, keepdims=True)
        pair = 2 * step + i
        send_ref[pl.ds(4 * pair, 4), 0:16, :] = state.reshape(4, 16, 128)
        for t in range(32):
            send_ref[t, pl.ds(16 + pair, 1), :] = norm


def project(x, dy, w_qkv, w_out):
    rows, width = x.shape
    whole = pl.BlockSpec((rows, width), lambda i: (0, 0))
    column = lambda first: pl.BlockSpec((width, 256), lambda i: (0, first + i))
    out = pl.BlockSpec((rows, 256), lambda i: (0, i))
    return pl.pallas_call(
        project_kernel,
        grid=(3,),
        in_specs=[whole, whole, column(0), column(3), column(6), column(0)],
        out_specs=[out] * 4 + [pl.BlockSpec((32, 24, 128), lambda i: (0, 0, 0))],
        out_shape=[jax.ShapeDtypeStruct((rows, INNER), BF16)] * 4
        + [jax.ShapeDtypeStruct((32, 24, 128), F32)],
        compiler_params=pltpu.CompilerParams(vmem_limit_bytes=VMEM_LIMIT),
        name="project",
    )(x, dy, w_qkv, w_qkv, w_qkv, w_out)


def denominators_kernel(me_ref, got_ref, q_ref, k_ref, g_ref, send_ref, den_ref, norm_ref, w_ref):
    me = me_ref[0]
    carry = jnp.zeros((16, 128), F32)
    norms = jnp.zeros((8, 128), F32)
    for t in range(32):
        send_ref[t, 0:16, :] = carry
        carry = carry + got_ref[t, 0:16, :]
        norms = norms + jnp.where(t < me, got_ref[t, 16:24, :], 0.0)
    norm_ref[...] = norms
    mask = causal()
    for p in range(PAIRS):
        lanes = slice(128 * p, 128 * p + 128)
        fq32 = features(q_ref[:, lanes].astype(F32))
        fq = fq32.astype(BF16)
        fk = features(k_ref[:, lanes].astype(F32)).astype(BF16)
        fq_norm = fq.astype(F32) * norms[p : p + 1, :]
        sums = []
        for half, (rows, extra) in enumerate(zip(split_pair(fq), split_pair(fq_norm))):
            scores = jnp.where(mask, mm_bt(rows, fk), 0.0)
            w_ref[p, :, 128 * half : 128 * half + 128] = scores.astype(BF16)
            sums.append(jnp.sum(scores + extra, axis=1, keepdims=True))
        den = jnp.where(low_lanes((BLOCK, 128)), sums[0], sums[1])
        den_ref[:, lanes] = den
        dnum = (g_ref[:, lanes].astype(F32) / den).astype(BF16)
        dstate = diagonal_blocks(mm_at(fq, dnum))
        send_ref[4 * p : 4 * p + 4, 16:32, :] = dstate.reshape(4, 16, 128)
    send_ref[24:32, 16:32, :] = jnp.zeros((8, 16, 128), F32)


def in_vmem(n):
    return [pl.BlockSpec(memory_space=pltpu.VMEM)] * n


SCALARS = pl.BlockSpec(memory_space=pltpu.SMEM)


def denominators(me, got, q, k, g):
    return pl.pallas_call(
        denominators_kernel,
        in_specs=[SCALARS] + in_vmem(4),
        out_specs=in_vmem(4),
        out_shape=[
            jax.ShapeDtypeStruct((32, 32, 128), F32),
            jax.ShapeDtypeStruct((BLOCK, INNER), F32),
            jax.ShapeDtypeStruct((8, 128), F32),
            jax.ShapeDtypeStruct((PAIRS, BLOCK, 256), BF16),
        ],
        compiler_params=pltpu.CompilerParams(vmem_limit_bytes=VMEM_LIMIT),
        name="denominators",
    )(me, got, q, k, g)


def forward_kernel(
    got_ref, q_ref, k_ref, v_ref, g_ref, den_ref, norm_ref, w_ref, send_ref, out_ref, dq_ref, ds_ref
):
    carry = jnp.zeros((16, 128), F32)
    for t in reversed(range(32)):
        send_ref[t, 0:16, :] = carry
        carry = carry + got_ref[t, 16:32, :]
    mask = causal()
    low = low_lanes((BLOCK, 128))
    dnorms = []
    for p in range(PAIRS):
        lanes = slice(128 * p, 128 * p + 128)
        block, part = p // 3, slice(128 * (p % 3), 128 * (p % 3) + 128)
        q = q_ref[:, lanes].astype(F32)
        fq = features(q).astype(BF16)
        fk = features(k_ref[:, lanes].astype(F32)).astype(BF16)
        v = v_ref[:, lanes]
        g = g_ref[:, lanes].astype(F32)
        inverse = 1.0 / den_ref[:, lanes]
        state = block_diagonal(got_ref[4 * p : 4 * p + 4, 0:16, :].reshape(64, 128).astype(BF16))
        v_halves = jnp.concatenate(split_pair(v), axis=0)
        ratio = (mm(w_ref[p], v_halves) + mm(fq, state)) * inverse
        out_ref[2 + block, :, part] = ratio.astype(BF16).astype(F32)
        dnum = (g * inverse).astype(BF16)
        sums = [jnp.sum(a, axis=1, keepdims=True) for a in split_pair(g * ratio)]
        dden = -jnp.where(low, sums[0], sums[1]) * inverse
        ddens = (dden[:, 0:1], dden[:, 127:128])
        dnorms.append(jnp.sum(dden * fq.astype(F32), axis=0, keepdims=True))
        ds = [
            jnp.where(mask, mm_bt(rows, v) + column, 0.0).astype(BF16)
            for rows, column in zip(split_pair(dnum), ddens)
        ]
        ds_ref[p] = jnp.concatenate(ds, axis=0)
        dfq = (
            mm(jnp.concatenate(ds, axis=1), jnp.concatenate(split_pair(fk), axis=0))
            + mm_bt(dnum, state)
            + dden * norm_ref[p : p + 1, :]
        )
        dq = (dfq * slope(q)).astype(BF16)
        dq_ref[:, lanes] = dq
        out_ref[block, :, part] = dq.astype(F32)
    dnorm = jnp.concatenate(dnorms + [jnp.zeros((2, 128), F32)], axis=0)
    for t in range(32):
        send_ref[t, 16:24, :] = dnorm


def forward(got, q, k, v, g, den, norm, w):
    return pl.pallas_call(
        forward_kernel,
        in_specs=in_vmem(8),
        out_specs=in_vmem(4),
        out_shape=[
            jax.ShapeDtypeStruct((32, 24, 128), F32),
            jax.ShapeDtypeStruct((4, BLOCK, 384), F32),
            jax.ShapeDtypeStruct((BLOCK, INNER), BF16),
            jax.ShapeDtypeStruct((PAIRS, 256, 128), BF16),
        ],
        compiler_params=pltpu.CompilerParams(vmem_limit_bytes=VMEM_LIMIT),
        name="forward",
    )(got, q, k, v, g, den, norm, w)


def backward_kernel(
    me_ref, got_ref, q_ref, k_ref, v_ref, g_ref, den_ref, w_ref, ds_ref, out_ref, dkv_ref
):
    me = me_ref[0]
    dnorms = jnp.zeros((8, 128), F32)
    for t in range(32):
        dnorms = dnorms + jnp.where(t > me, got_ref[t, 16:24, :], 0.0)
    for p in range(PAIRS):
        lanes = slice(128 * p, 128 * p + 128)
        block, part = p // 3, slice(128 * (p % 3), 128 * (p % 3) + 128)
        fq = features(q_ref[:, lanes].astype(F32)).astype(BF16)
        k = k_ref[:, lanes].astype(F32)
        fk = features(k).astype(BF16)
        v = v_ref[:, lanes]
        dnum = (g_ref[:, lanes].astype(F32) * (1.0 / den_ref[:, lanes])).astype(BF16)
        dstate = block_diagonal(got_ref[4 * p : 4 * p + 4, 0:16, :].reshape(64, 128).astype(BF16))
        dfk = (
            mm_at(ds_ref[p], jnp.concatenate(split_pair(fq), axis=0))
            + mm_bt(v, dstate)
            + dnorms[p : p + 1, :]
        )
        dk = (dfk * slope(k)).astype(BF16)
        w = jnp.concatenate([w_ref[p, :, 0:128], w_ref[p, :, 128:256]], axis=0)
        dv = (mm_at(w, jnp.concatenate(split_pair(dnum), axis=0)) + mm(fk, dstate)).astype(BF16)
        out_ref[block, :, part] = dk.astype(F32)
        out_ref[2 + block, :, part] = dv.astype(F32)
        dkv_ref[:, lanes] = dk
        dkv_ref[:, slice(INNER + 128 * p, INNER + 128 * p + 128)] = dv


def backward(me, got, q, k, v, g, den, w, ds):
    return pl.pallas_call(
        backward_kernel,
        in_specs=[SCALARS] + in_vmem(8),
        out_specs=in_vmem(2),
        out_shape=[
            jax.ShapeDtypeStruct((4, BLOCK, 384), F32),
            jax.ShapeDtypeStruct((BLOCK, 2 * INNER), BF16),
        ],
        compiler_params=pltpu.CompilerParams(vmem_limit_bytes=VMEM_LIMIT),
        name="backward",
    )(me, got, q, k, v, g, den, w, ds)


def weights_kernel(y_ref, xdy_ref, first_ref, second_ref, out_ref):
    y = y_ref[0]
    columns = xdy_ref.shape[-1]
    x = xdy_ref[:, 0].reshape(4 * BLOCK, columns).astype(BF16)
    other = xdy_ref[:, y // 2].reshape(4 * BLOCK, columns).astype(BF16)
    first = mm_at(other, first_ref[...].reshape(4 * BLOCK, 384).astype(BF16))
    second = mm_at(x, second_ref[...].reshape(4 * BLOCK, 384).astype(BF16))
    blocks = columns // 32
    first = first.reshape(blocks, 2, 16, 384)
    second = second.reshape(blocks, 2, 16, 384)
    for c in range(2):
        out_ref[c, :, :, 0:384] = first[:, c]
        out_ref[c, :, :, 384:768] = second[:, c]


def weights(y, xdy, first, second):
    blocks = pl.BlockSpec((4, BLOCK, 384), lambda i: (0, 0, 0))
    return pl.pallas_call(
        weights_kernel,
        grid=(4,),
        in_specs=[
            SCALARS,
            pl.BlockSpec((4, 2, BLOCK, 256), lambda i: (0, 0, 0, i)),
            blocks,
            blocks,
        ],
        out_specs=pl.BlockSpec((2, 8, 16, 768), lambda i: (0, i, 0, 0)),
        out_shape=jax.ShapeDtypeStruct((2, 32, 16, 768), F32),
        compiler_params=pltpu.CompilerParams(vmem_limit_bytes=VMEM_LIMIT),
        name="weights",
    )(y, xdy, first, second)


def swap(a, axes):
    return lax.all_to_all(a, axes, 0, 0, tiled=True)


def per_device(frames, grad_frames, w_qkv, w_out):
    x = frames[0]
    dy = grad_frames[0]
    me = lax.axis_index(TM).reshape(1).astype(jnp.int32)
    y = lax.axis_index("y").reshape(1).astype(jnp.int32)
    xdy = lax.all_gather(jnp.stack([x.astype(F32), dy.astype(F32)]), "y")
    q, k, v, g, send = project(x, dy, w_qkv, w_out)
    got = swap(send, TM)
    send, den, norm, w = denominators(me, got, q, k, g)
    got = swap(send, TM)
    send, first, dq, ds = forward(got, q, k, v, g, den, norm, w)
    got = swap(send, TM)
    second, dkv = backward(me, got, q, k, v, g, den, w, ds)
    dqkv = jnp.concatenate([dq, dkv], axis=1)
    dx = lax.dot_general(dqkv, w_qkv, (((1,), (1,)), ((), ())), preferred_element_type=F32).astype(BF16)
    first = swap(first, "y")
    second = swap(second, "y")
    part = swap(weights(y, xdy, first, second), "c")
    part = part[0] + part[1]
    total = jnp.sum(swap(part, TM), axis=0)
    pieces = swap(jnp.broadcast_to(total[None], (8,) + total.shape), DP)
    pieces = pieces.reshape(4, 32, 768)
    half = 384
    grad_qkv = jnp.concatenate(
        [pieces[0, :, :half], pieces[1, :, :half]] + [pieces[i, :, half:] for i in range(4)], axis=1
    )
    grad_out = jnp.concatenate([pieces[2, :, :half], pieces[3, :, :half]], axis=1)
    return dx[None], grad_qkv, grad_out


def solution(mesh):
    torus = Mesh(mesh.devices.reshape(8, 4, 4, 2), TM + DP)
    rows = P(DP, TM, None)
    return jax.shard_map(
        per_device,
        mesh=torus,
        in_specs=(rows, rows, P(), P()),
        out_specs=(rows, P(TM, None), P(TM, None)),
        check_vma=False,
    )
```

```python
import functools

import jax
import jax.numpy as jnp
from jax import lax
from jax.experimental import pallas as pl
from jax.experimental.pallas import tpu as pltpu
from jax.sharding import Mesh
from jax.sharding import PartitionSpec as P

HEADS = 12
HEAD = 64
BLOCK = 128
PAIRS = HEADS // 2
INNER = HEADS * HEAD
TM = ("z", "x")
DP = ("y", "c")
F32 = jnp.float32
BF16 = jnp.bfloat16
VMEM_LIMIT = 32 * 1024 * 1024
PROJECT_VMEM = 52000 * 1024
WEIGHTS_VMEM = 52000 * 1024


def features(a):
    return jnp.where(a > 0, a + 1.0, jnp.exp(jnp.minimum(a, 0.0)))


def slope(a):
    return jnp.where(a > 0, 1.0, jnp.exp(jnp.minimum(a, 0.0)))


def low_lanes(shape):
    return lax.broadcasted_iota(jnp.int32, shape, len(shape) - 1) < HEAD


def split_pair(a):
    low = low_lanes(a.shape)
    zero = jnp.zeros_like(a)
    return jnp.where(low, a, zero), jnp.where(low, zero, a)


def block_diagonal(packed):
    first, second = split_pair(packed)
    return jnp.concatenate([first, second], axis=0)


def diagonal_blocks(m):
    return jnp.where(low_lanes((HEAD, 2 * HEAD)), m[:HEAD], m[HEAD:])


def mm(a, b):
    return lax.dot_general(a, b, (((1,), (0,)), ((), ())), preferred_element_type=F32)


def mm_bt(a, b):
    return lax.dot_general(a, b, (((1,), (1,)), ((), ())), preferred_element_type=F32)


def mm_at(a, b):
    return lax.dot_general(a, b, (((0,), (0,)), ((), ())), preferred_element_type=F32)


def causal():
    rows = lax.broadcasted_iota(jnp.int32, (BLOCK, BLOCK), 0)
    columns = lax.broadcasted_iota(jnp.int32, (BLOCK, BLOCK), 1)
    return columns <= rows


def in_vmem(n):
    return [pl.BlockSpec(memory_space=pltpu.VMEM)] * n


def in_hbm(n):
    return [pl.BlockSpec(memory_space=pltpu.HBM)] * n


SCALARS = pl.BlockSpec(memory_space=pltpu.SMEM)


def project_kernel(
    x_hbm, dy_hbm, w_hbm, wo_hbm, q_ref, k_ref, v_ref, g_ref, send_ref, xdy_ref,
    x_ref, dy_ref, w_ref, wo_ref, frame_sem, weight_sem,
):
    frames = [
        pltpu.make_async_copy(x_hbm, x_ref, frame_sem.at[0]),
        pltpu.make_async_copy(dy_hbm, dy_ref, frame_sem.at[1]),
    ]
    for copy in frames:
        copy.start()
    copies = []
    for step in range(3):
        lanes = pl.ds(256 * step, 256)
        row = []
        for kind, first in ((1, INNER), (2, 2 * INNER), (0, 0)):
            columns = pl.ds(first + 256 * step, 256)
            sem = weight_sem.at[step, kind]
            row.append(pltpu.make_async_copy(w_hbm.at[:, columns], w_ref.at[:, columns], sem))
        row.append(pltpu.make_async_copy(wo_hbm.at[:, lanes], wo_ref.at[:, lanes], weight_sem.at[step, 3]))
        for copy in row:
            copy.start()
        copies.append(row)
    send_ref[24:32, 0:16, :] = jnp.zeros((8, 16, 128), F32)
    send_ref[:, 22:24, :] = jnp.zeros((32, 2, 128), F32)
    for copy in frames:
        copy.wait()
    x = x_ref[...]
    dy = dy_ref[...]
    xdy_ref[0] = x.astype(F32)
    xdy_ref[1] = dy.astype(F32)
    for step in range(3):
        k_copy, v_copy, q_copy, g_copy = copies[step]
        lanes = slice(256 * step, 256 * step + 256)
        k_copy.wait()
        k = mm(x, w_ref[:, slice(INNER + 256 * step, INNER + 256 * step + 256)]).astype(BF16)
        k_ref[:, lanes] = k
        v_copy.wait()
        v = mm(x, w_ref[:, slice(2 * INNER + 256 * step, 2 * INNER + 256 * step + 256)]).astype(BF16)
        v_ref[:, lanes] = v
        fk = features(k.astype(F32)).astype(BF16)
        for i in range(2):
            part = slice(128 * i, 128 * i + 128)
            state = diagonal_blocks(mm_at(fk[:, part], v[:, part]))
            norm = jnp.sum(fk[:, part].astype(F32), axis=0, keepdims=True)
            pair = 2 * step + i
            send_ref[4 * pair : 4 * pair + 4, 0:16, :] = state.reshape(4, 16, 128)
            for t in range(32):
                send_ref[t, 16 + pair : 17 + pair, :] = norm
        q_copy.wait()
        q_ref[:, lanes] = mm(x, w_ref[:, lanes]).astype(BF16)
        g_copy.wait()
        g_ref[:, lanes] = mm(dy, wo_ref[:, lanes]).astype(BF16)


def project(x, dy, w_qkv, w_out):
    rows, width = x.shape
    return pl.pallas_call(
        project_kernel,
        in_specs=in_hbm(4),
        out_specs=in_vmem(6),
        out_shape=[jax.ShapeDtypeStruct((rows, INNER), BF16)] * 4
        + [jax.ShapeDtypeStruct((32, 24, 128), F32), jax.ShapeDtypeStruct((2, rows, width), F32)],
        scratch_shapes=[
            pltpu.VMEM(x.shape, BF16),
            pltpu.VMEM(dy.shape, BF16),
            pltpu.VMEM(w_qkv.shape, BF16),
            pltpu.VMEM(w_out.shape, BF16),
            pltpu.SemaphoreType.DMA((2,)),
            pltpu.SemaphoreType.DMA((3, 4)),
        ],
        compiler_params=pltpu.CompilerParams(vmem_limit_bytes=PROJECT_VMEM),
        name="project",
    )(x, dy, w_qkv, w_out)


def denominators_kernel(me_ref, got_ref, q_ref, k_ref, g_ref, send_ref, den_ref, norm_ref, w_ref):
    me = me_ref[0]
    carry = jnp.zeros((16, 128), F32)
    norms = jnp.zeros((8, 128), F32)
    for t in range(32):
        send_ref[t, 0:16, :] = carry
        carry = carry + got_ref[t, 0:16, :]
        norms = norms + jnp.where(t < me, got_ref[t, 16:24, :], 0.0)
    norm_ref[...] = norms
    mask = causal()
    for p in range(PAIRS):
        lanes = slice(128 * p, 128 * p + 128)
        fq32 = features(q_ref[:, lanes].astype(F32))
        fq = fq32.astype(BF16)
        fk = features(k_ref[:, lanes].astype(F32)).astype(BF16)
        fq_norm = fq.astype(F32) * norms[p : p + 1, :]
        sums = []
        for half, (rows, extra) in enumerate(zip(split_pair(fq), split_pair(fq_norm))):
            scores = jnp.where(mask, mm_bt(rows, fk), 0.0)
            w_ref[p, :, 128 * half : 128 * half + 128] = scores.astype(BF16)
            sums.append(jnp.sum(scores + extra, axis=1, keepdims=True))
        den = jnp.where(low_lanes((BLOCK, 128)), sums[0], sums[1])
        den_ref[:, lanes] = den
        dnum = (g_ref[:, lanes].astype(F32) / den).astype(BF16)
        dstate = diagonal_blocks(mm_at(fq, dnum))
        send_ref[4 * p : 4 * p + 4, 16:32, :] = dstate.reshape(4, 16, 128)
    send_ref[24:32, 16:32, :] = jnp.zeros((8, 16, 128), F32)


def denominators(me, got, q, k, g):
    return pl.pallas_call(
        denominators_kernel,
        in_specs=[SCALARS] + in_vmem(4),
        out_specs=in_vmem(4),
        out_shape=[
            jax.ShapeDtypeStruct((32, 32, 128), F32),
            jax.ShapeDtypeStruct((BLOCK, INNER), F32),
            jax.ShapeDtypeStruct((8, 128), F32),
            jax.ShapeDtypeStruct((PAIRS, BLOCK, 256), BF16),
        ],
        compiler_params=pltpu.CompilerParams(vmem_limit_bytes=VMEM_LIMIT),
        name="denominators",
    )(me, got, q, k, g)


def forward_kernel(
    y_ref, got_ref, q_ref, k_ref, v_ref, g_ref, den_ref, norm_ref, w_ref, send_ref, dq_ref, ds_ref, *rest
):
    *block_refs, out_ref = rest
    carry = jnp.zeros((16, 128), F32)
    for t in reversed(range(32)):
        send_ref[t, 0:16, :] = carry
        carry = carry + got_ref[t, 16:32, :]
    mask = causal()
    low = low_lanes((BLOCK, 128))
    dnorms = []
    for p in range(PAIRS):
        lanes = slice(128 * p, 128 * p + 128)
        block, part = p // 3, slice(128 * (p % 3), 128 * (p % 3) + 128)
        q = q_ref[:, lanes].astype(F32)
        fq = features(q).astype(BF16)
        fk = features(k_ref[:, lanes].astype(F32)).astype(BF16)
        v = v_ref[:, lanes]
        g = g_ref[:, lanes].astype(F32)
        inverse = 1.0 / den_ref[:, lanes]
        state = block_diagonal(got_ref[4 * p : 4 * p + 4, 0:16, :].reshape(64, 128).astype(BF16))
        v_halves = jnp.concatenate(split_pair(v), axis=0)
        ratio = (mm(w_ref[p], v_halves) + mm(fq, state)) * inverse
        out_ref[2 + block, :, part] = ratio.astype(BF16).astype(F32)
        dnum = (g * inverse).astype(BF16)
        sums = [jnp.sum(a, axis=1, keepdims=True) for a in split_pair(g * ratio)]
        dden = -jnp.where(low, sums[0], sums[1]) * inverse
        ddens = (dden[:, 0:1], dden[:, 127:128])
        dnorms.append(jnp.sum(dden * fq.astype(F32), axis=0, keepdims=True))
        ds = [
            jnp.where(mask, mm_bt(rows, v) + column, 0.0).astype(BF16)
            for rows, column in zip(split_pair(dnum), ddens)
        ]
        ds_ref[p] = jnp.concatenate(ds, axis=0)
        dfq = (
            mm(jnp.concatenate(ds, axis=1), jnp.concatenate(split_pair(fk), axis=0))
            + mm_bt(dnum, state)
            + dden * norm_ref[p : p + 1, :]
        )
        dq = (dfq * slope(q)).astype(BF16)
        dq_ref[:, lanes] = dq
        out_ref[block, :, part] = dq.astype(F32)
    dnorm = jnp.concatenate(dnorms + [jnp.zeros((2, 128), F32)], axis=0)
    for t in range(32):
        send_ref[t, 16:24, :] = dnorm
    for s, block_ref in enumerate(block_refs):
        block_ref[...] = out_ref[lax.rem(y_ref[0] + s, 4)]


def forward(y, got, q, k, v, g, den, norm, w):
    return pl.pallas_call(
        forward_kernel,
        in_specs=[SCALARS] + in_vmem(8),
        out_specs=in_vmem(7),
        out_shape=[
            jax.ShapeDtypeStruct((32, 24, 128), F32),
            jax.ShapeDtypeStruct((BLOCK, INNER), BF16),
            jax.ShapeDtypeStruct((PAIRS, 256, 128), BF16),
        ]
        + [jax.ShapeDtypeStruct((BLOCK, 384), F32)] * 4,
        scratch_shapes=[pltpu.VMEM((4, BLOCK, 384), F32)],
        compiler_params=pltpu.CompilerParams(vmem_limit_bytes=VMEM_LIMIT),
        name="forward",
    )(y, got, q, k, v, g, den, norm, w)


def backward_kernel(
    me_ref, got_ref, q_ref, k_ref, v_ref, g_ref, den_ref, w_ref, ds_ref, out_ref, dkv_ref
):
    me = me_ref[0]
    dnorms = jnp.zeros((8, 128), F32)
    for t in range(32):
        dnorms = dnorms + jnp.where(t > me, got_ref[t, 16:24, :], 0.0)
    for p in range(PAIRS):
        lanes = slice(128 * p, 128 * p + 128)
        block, part = p // 3, slice(128 * (p % 3), 128 * (p % 3) + 128)
        fq = features(q_ref[:, lanes].astype(F32)).astype(BF16)
        k = k_ref[:, lanes].astype(F32)
        fk = features(k).astype(BF16)
        v = v_ref[:, lanes]
        dnum = (g_ref[:, lanes].astype(F32) * (1.0 / den_ref[:, lanes])).astype(BF16)
        dstate = block_diagonal(got_ref[4 * p : 4 * p + 4, 0:16, :].reshape(64, 128).astype(BF16))
        dfk = (
            mm_at(ds_ref[p], jnp.concatenate(split_pair(fq), axis=0))
            + mm_bt(v, dstate)
            + dnorms[p : p + 1, :]
        )
        dk = (dfk * slope(k)).astype(BF16)
        w = jnp.concatenate([w_ref[p, :, 0:128], w_ref[p, :, 128:256]], axis=0)
        dv = (mm_at(w, jnp.concatenate(split_pair(dnum), axis=0)) + mm(fk, dstate)).astype(BF16)
        out_ref[block, :, part] = dk.astype(F32)
        out_ref[2 + block, :, part] = dv.astype(F32)
        dkv_ref[:, lanes] = dk
        dkv_ref[:, slice(INNER + 128 * p, INNER + 128 * p + 128)] = dv


def backward(me, got, q, k, v, g, den, w, ds):
    return pl.pallas_call(
        backward_kernel,
        in_specs=[SCALARS] + in_vmem(8),
        out_specs=in_vmem(2),
        out_shape=[
            jax.ShapeDtypeStruct((4, BLOCK, 384), F32),
            jax.ShapeDtypeStruct((BLOCK, 2 * INNER), BF16),
        ],
        compiler_params=pltpu.CompilerParams(vmem_limit_bytes=VMEM_LIMIT),
        name="backward",
    )(me, got, q, k, v, g, den, w, ds)


def weights_kernel(where_ref, choice_ref, xdy_hbm, blocks_ref, keep_ref, send_ref, xdy_ref, sems, *, relative):
    y = where_ref[0]
    c = where_ref[1]
    choice = choice_ref[0]
    copies = []
    for j in range(4):
        lanes = pl.ds(256 * j, 256)
        copies.append(
            pltpu.make_async_copy(xdy_hbm.at[:, choice, :, lanes], xdy_ref.at[:, :, lanes], sems.at[j])
        )
        copies[-1].start()
    order = [lax.rem(y + 4 - s, 4) if relative else s for s in range(4)]
    blocks = [r[...] for r in blocks_ref] if relative else [blocks_ref[0][s] for s in range(4)]
    blocks = jnp.concatenate(blocks, axis=0).astype(BF16)
    for j in range(4):
        copies[j].wait()
        x = jnp.concatenate([xdy_ref[i, :, 256 * j : 256 * j + 256] for i in order], axis=0).astype(BF16)
        part = mm_at(x, blocks).reshape(2, 4, 2, 16, 384)
        for i in range(4):
            first, second = part[:, i, 0], part[:, i, 1]
            keep_ref[i, 2 * j : 2 * j + 2] = jnp.where(c == 0, first, second)
            send_ref[i, 2 * j : 2 * j + 2] = jnp.where(c == 0, second, first)


def weights(where, choice, xdy, blocks):
    relative = len(blocks) == 4

    def kernel(*refs):
        n = len(blocks)
        weights_kernel(*refs[:3], refs[3 : 3 + n], *refs[3 + n :], relative=relative)

    out = jax.ShapeDtypeStruct((4, 8, 16, 384), F32)
    return pl.pallas_call(
        kernel,
        in_specs=[SCALARS, SCALARS] + in_hbm(1) + in_vmem(len(blocks)),
        out_specs=in_vmem(2),
        out_shape=[out, out],
        scratch_shapes=[pltpu.VMEM((4, BLOCK, 1024), F32), pltpu.SemaphoreType.DMA((4,))],
        compiler_params=pltpu.CompilerParams(vmem_limit_bytes=WEIGHTS_VMEM),
        name="weights",
    )(where, choice, xdy, *blocks)


def pair_sum_kernel(x_ref, keep_ref, got_ref, *out_refs):
    for s, out_ref in enumerate(out_refs):
        i = lax.rem(x_ref[0] + s, 4)
        out_ref[...] = keep_ref[i] + got_ref[i]


def pair_sum(x, keep, got):
    return pl.pallas_call(
        pair_sum_kernel,
        in_specs=[SCALARS] + in_vmem(2),
        out_specs=in_vmem(4),
        out_shape=[jax.ShapeDtypeStruct((8, 16, 384), F32)] * 4,
        compiler_params=pltpu.CompilerParams(vmem_limit_bytes=VMEM_LIMIT),
        name="pair_sum",
    )(x, keep, got)


def merge_kernel(own_ref, a_ref, b_ref, c_ref, second_ref, out_ref):
    out_ref[:, :, 0:384] = (own_ref[...] + a_ref[...]) + (b_ref[...] + c_ref[...])
    out_ref[:, :, 384:768] = (second_ref[0] + second_ref[1]) + (second_ref[2] + second_ref[3])


def merge(first, second):
    return pl.pallas_call(
        merge_kernel,
        in_specs=in_vmem(5),
        out_specs=in_vmem(1)[0],
        out_shape=jax.ShapeDtypeStruct((8, 16, 768), F32),
        compiler_params=pltpu.CompilerParams(vmem_limit_bytes=VMEM_LIMIT),
        name="merge",
    )(*first, second)


def spread_kernel(got_ref, out_ref):
    total = got_ref[0]
    for i in range(1, 8):
        total = total + got_ref[i]
    for i in range(8):
        out_ref[i] = total


def spread(got):
    return pl.pallas_call(
        spread_kernel,
        in_specs=in_vmem(1),
        out_specs=in_vmem(1)[0],
        out_shape=jax.ShapeDtypeStruct(got.shape, F32),
        compiler_params=pltpu.CompilerParams(vmem_limit_bytes=VMEM_LIMIT),
        name="spread",
    )(got)


def assemble_kernel(got_ref, qkv_ref, out_ref):
    for y in range(4):
        for c in range(2):
            rows = slice(16 * c, 16 * c + 16)
            piece = got_ref[2 * y + c]
            target = qkv_ref if y < 2 else out_ref
            target[rows, 384 * (y % 2) : 384 * (y % 2) + 384] = piece[:, 0:384]
            qkv_ref[rows, INNER + 384 * y : INNER + 384 * y + 384] = piece[:, 384:768]


def assemble(got):
    return pl.pallas_call(
        assemble_kernel,
        in_specs=in_vmem(1),
        out_specs=in_vmem(2),
        out_shape=[jax.ShapeDtypeStruct((32, 3 * INNER), F32), jax.ShapeDtypeStruct((32, INNER), F32)],
        compiler_params=pltpu.CompilerParams(vmem_limit_bytes=VMEM_LIMIT),
        name="assemble",
    )(got)


def swap(a, axes):
    return lax.all_to_all(a, axes, 0, 0, tiled=True)


def rotate(blocks, axis):
    n = len(blocks)
    moved = [lax.ppermute(b, axis, [(i, (i + s) % n) for i in range(n)]) for s, b in enumerate(blocks) if s]
    return [blocks[0]] + moved


def other_core(a):
    return lax.ppermute(a, "c", [(0, 1), (1, 0)])


def scalars(*values):
    return jnp.stack([jnp.asarray(v, jnp.int32) for v in values])


def per_device(frames, grad_frames, w_qkv, w_out):
    me = scalars(lax.axis_index(TM))
    y, c = lax.axis_index("y"), lax.axis_index("c")
    where = scalars(y, c)
    q, k, v, g, send, xdy = project(frames[0], grad_frames[0], w_qkv, w_out)
    xdy = lax.all_gather(xdy, "y")
    got = swap(send, TM)
    send, den, norm, w = denominators(me, got, q, k, g)
    got = swap(send, TM)
    send, dq, ds, *first = forward(scalars(y), got, q, k, v, g, den, norm, w)
    first = rotate(first, "y")
    got = swap(send, TM)
    keep, give = weights(where, scalars(y // 2), xdy, first)
    got, give = lax.optimization_barrier((got, give))
    second, dkv = backward(me, got, q, k, v, g, den, w, ds)
    dqkv = jnp.concatenate([dq, dkv], axis=1)
    dx = lax.dot_general(dqkv, w_qkv, (((1,), (1,)), ((), ())), preferred_element_type=F32).astype(BF16)
    first = pair_sum(scalars(lax.axis_index("x")), keep, other_core(give))
    first = rotate(first, "x")
    second, first = lax.optimization_barrier((swap(second, "y"), first))
    keep, give = weights(where, scalars(0), xdy, [second])
    part = merge(first, swap(keep + other_core(give), "x"))
    grad_qkv, grad_out = assemble(swap(spread(swap(part, "z")), DP))
    return dx[None], grad_qkv, grad_out


def solution(mesh):
    torus = Mesh(mesh.devices.reshape(8, 4, 4, 2), TM + DP)
    rows = P(DP, TM, None)
    return jax.shard_map(
        per_device,
        mesh=torus,
        in_specs=(rows, rows, P(), P()),
        out_specs=(rows, P(TM, None), P(TM, None)),
        check_vma=False,
    )
```

```python
import jax
import jax.numpy as jnp
from jax import lax
from jax.experimental import pallas as pl
from jax.experimental.pallas import tpu as pltpu
from jax.sharding import Mesh
from jax.sharding import PartitionSpec as P

HEADS = 12
HEAD = 64
BLOCK = 128
PAIRS = HEADS // 2
INNER = HEADS * HEAD
TM = ("z", "x")
DP = ("y", "c")
F32 = jnp.float32
BF16 = jnp.bfloat16
VMEM_LIMIT = 32 * 1024 * 1024
LARGE_VMEM = 54300 * 1024


def features(a):
    return jnp.where(a > 0, a + 1.0, jnp.exp(jnp.minimum(a, 0.0)))


def slope(a):
    return jnp.where(a > 0, 1.0, jnp.exp(jnp.minimum(a, 0.0)))


def low_lanes(shape):
    return lax.broadcasted_iota(jnp.int32, shape, len(shape) - 1) < HEAD


def split_pair(a):
    low = low_lanes(a.shape)
    zero = jnp.zeros_like(a)
    return jnp.where(low, a, zero), jnp.where(low, zero, a)


def block_diagonal(packed):
    first, second = split_pair(packed)
    return jnp.concatenate([first, second], axis=0)


def diagonal_blocks(m):
    return jnp.where(low_lanes((HEAD, 2 * HEAD)), m[:HEAD], m[HEAD:])


def mm(a, b):
    return lax.dot_general(a, b, (((1,), (0,)), ((), ())), preferred_element_type=F32)


def mm_bt(a, b):
    return lax.dot_general(a, b, (((1,), (1,)), ((), ())), preferred_element_type=F32)


def mm_at(a, b):
    return lax.dot_general(a, b, (((0,), (0,)), ((), ())), preferred_element_type=F32)


def causal():
    rows = lax.broadcasted_iota(jnp.int32, (BLOCK, BLOCK), 0)
    columns = lax.broadcasted_iota(jnp.int32, (BLOCK, BLOCK), 1)
    return columns <= rows


def in_vmem(n):
    return [pl.BlockSpec(memory_space=pltpu.VMEM)] * n


def in_hbm(n):
    return [pl.BlockSpec(memory_space=pltpu.HBM)] * n


def f32(*shape):
    return jax.ShapeDtypeStruct(shape, F32)


def bf16(*shape):
    return jax.ShapeDtypeStruct(shape, BF16)


def call(kernel, args, outs, name, scratch=(), in_specs=None, limit=VMEM_LIMIT):
    return pl.pallas_call(
        kernel,
        in_specs=in_specs or in_vmem(len(args)),
        out_specs=in_vmem(len(outs)),
        out_shape=outs,
        scratch_shapes=list(scratch),
        compiler_params=pltpu.CompilerParams(vmem_limit_bytes=limit),
        name=name,
    )(*args)


def time_index():
    return lax.axis_index("z") * 4 + lax.axis_index("x")


def project_kernel(
    x_hbm, dy_hbm, w_hbm, wo_hbm, q_ref, k_ref, v_ref, g_ref, send_ref, xdy_ref,
    x_ref, dy_ref, w_ref, wo_ref, frame_sem, weight_sem,
):
    frames = [
        pltpu.make_async_copy(x_hbm, x_ref, frame_sem.at[0]),
        pltpu.make_async_copy(dy_hbm, dy_ref, frame_sem.at[1]),
    ]
    for copy in frames:
        copy.start()

    def fetch(step):
        copies = []
        for kind, first in enumerate((INNER, 2 * INNER, 0)):
            columns = pl.ds(first + 256 * step, 256)
            sem = weight_sem.at[step, kind]
            copies.append(pltpu.make_async_copy(w_hbm.at[:, columns], w_ref.at[:, columns], sem))
        lanes = pl.ds(256 * step, 256)
        copies.append(pltpu.make_async_copy(wo_hbm.at[:, lanes], wo_ref.at[:, lanes], weight_sem.at[step, 3]))
        for copy in copies:
            copy.start()
        return copies

    copies = fetch(0)
    send_ref[24:32, 0:16, :] = jnp.zeros((8, 16, 128), F32)
    send_ref[:, 22:24, :] = jnp.zeros((32, 2, 128), F32)
    for copy in frames:
        copy.wait()
    x = x_ref[...]
    dy = dy_ref[...]
    xdy_ref[0] = x.astype(F32)
    xdy_ref[1] = dy.astype(F32)
    for step in range(3):
        lanes = slice(256 * step, 256 * step + 256)
        for copy in copies:
            copy.wait()
        if step < 2:
            copies = fetch(step + 1)
        k = mm(x, w_ref[:, slice(INNER + 256 * step, INNER + 256 * step + 256)]).astype(BF16)
        k_ref[:, lanes] = k
        v = mm(x, w_ref[:, slice(2 * INNER + 256 * step, 2 * INNER + 256 * step + 256)]).astype(BF16)
        v_ref[:, lanes] = v
        fk = features(k.astype(F32)).astype(BF16)
        for i in range(2):
            part = slice(128 * i, 128 * i + 128)
            state = diagonal_blocks(mm_at(fk[:, part], v[:, part]))
            norm = jnp.sum(fk[:, part].astype(F32), axis=0, keepdims=True)
            pair = 2 * step + i
            send_ref[4 * pair : 4 * pair + 4, 0:16, :] = state.reshape(4, 16, 128)
            for t in range(32):
                send_ref[t, 16 + pair : 17 + pair, :] = norm
        q_ref[:, lanes] = mm(x, w_ref[:, lanes]).astype(BF16)
        g_ref[:, lanes] = mm(dy, wo_ref[:, lanes]).astype(BF16)


def project(x, dy, w_qkv, w_out):
    rows, width = x.shape
    scratch = [pltpu.VMEM(a.shape, BF16) for a in (x, dy, w_qkv, w_out)]
    scratch += [pltpu.SemaphoreType.DMA((2,)), pltpu.SemaphoreType.DMA((3, 4))]
    outs = [bf16(rows, INNER)] * 4 + [f32(32, 24, 128), f32(2, rows, width)]
    return call(
        project_kernel, (x, dy, w_qkv, w_out), outs, "project", scratch, in_hbm(4), LARGE_VMEM
    )


def denominators_kernel(got_ref, q_ref, k_ref, g_ref, send_ref, den_ref, norm_ref, w_ref):
    me = time_index()
    carry = jnp.zeros((16, 128), F32)
    norms = jnp.zeros((8, 128), F32)
    for t in range(32):
        send_ref[t, 0:16, :] = carry
        carry = carry + got_ref[t, 0:16, :]
        norms = norms + jnp.where(t < me, got_ref[t, 16:24, :], 0.0)
    norm_ref[...] = norms
    mask = causal()
    for p in range(PAIRS):
        lanes = slice(128 * p, 128 * p + 128)
        fq32 = features(q_ref[:, lanes].astype(F32))
        fq = fq32.astype(BF16)
        fk = features(k_ref[:, lanes].astype(F32)).astype(BF16)
        fq_norm = fq.astype(F32) * norms[p : p + 1, :]
        sums = []
        for half, (rows, extra) in enumerate(zip(split_pair(fq), split_pair(fq_norm))):
            scores = jnp.where(mask, mm_bt(rows, fk), 0.0)
            w_ref[p, :, 128 * half : 128 * half + 128] = scores.astype(BF16)
            sums.append(jnp.sum(scores + extra, axis=1, keepdims=True))
        den = jnp.where(low_lanes((BLOCK, 128)), sums[0], sums[1])
        den_ref[:, lanes] = den
        dnum = (g_ref[:, lanes].astype(F32) / den).astype(BF16)
        dstate = diagonal_blocks(mm_at(fq, dnum))
        send_ref[4 * p : 4 * p + 4, 16:32, :] = dstate.reshape(4, 16, 128)
    send_ref[24:32, 16:32, :] = jnp.zeros((8, 16, 128), F32)


def denominators(*args):
    outs = [f32(32, 32, 128), f32(BLOCK, INNER), f32(8, 128), bf16(PAIRS, BLOCK, 256)]
    return call(denominators_kernel, args, outs, "denominators")


def forward_kernel(
    got_ref, q_ref, k_ref, v_ref, g_ref, den_ref, norm_ref, w_ref,
    send_ref, dq_ref, ds_ref, b0_ref, b1_ref, b2_ref, b3_ref, out_ref,
):
    carry = jnp.zeros((16, 128), F32)
    for t in reversed(range(32)):
        send_ref[t, 0:16, :] = carry
        carry = carry + got_ref[t, 16:32, :]
    mask = causal()
    low = low_lanes((BLOCK, 128))
    dnorms = []
    for p in range(PAIRS):
        lanes = slice(128 * p, 128 * p + 128)
        block, part = p // 3, slice(128 * (p % 3), 128 * (p % 3) + 128)
        q = q_ref[:, lanes].astype(F32)
        fq = features(q).astype(BF16)
        fk = features(k_ref[:, lanes].astype(F32)).astype(BF16)
        v = v_ref[:, lanes]
        g = g_ref[:, lanes].astype(F32)
        inverse = 1.0 / den_ref[:, lanes]
        state = block_diagonal(got_ref[4 * p : 4 * p + 4, 0:16, :].reshape(64, 128).astype(BF16))
        v_halves = jnp.concatenate(split_pair(v), axis=0)
        ratio = (mm(w_ref[p], v_halves) + mm(fq, state)) * inverse
        out_ref[2 + block, :, part] = ratio.astype(BF16).astype(F32)
        dnum = (g * inverse).astype(BF16)
        sums = [jnp.sum(a, axis=1, keepdims=True) for a in split_pair(g * ratio)]
        dden = -jnp.where(low, sums[0], sums[1]) * inverse
        ddens = (dden[:, 0:1], dden[:, 127:128])
        dnorms.append(jnp.sum(dden * fq.astype(F32), axis=0, keepdims=True))
        ds = [
            jnp.where(mask, mm_bt(rows, v) + column, 0.0).astype(BF16)
            for rows, column in zip(split_pair(dnum), ddens)
        ]
        ds_ref[p] = jnp.concatenate(ds, axis=0)
        dfq = (
            mm(jnp.concatenate(ds, axis=1), jnp.concatenate(split_pair(fk), axis=0))
            + mm_bt(dnum, state)
            + dden * norm_ref[p : p + 1, :]
        )
        dq = (dfq * slope(q)).astype(BF16)
        dq_ref[:, lanes] = dq
        out_ref[block, :, part] = dq.astype(F32)
    dnorm = jnp.concatenate(dnorms + [jnp.zeros((2, 128), F32)], axis=0)
    for t in range(32):
        send_ref[t, 16:24, :] = dnorm
    y = lax.axis_index("y")
    for i, ref in enumerate((b0_ref, b1_ref, b2_ref, b3_ref)):
        ref[...] = out_ref[lax.rem(y + i, 4)]


def forward(*args):
    outs = [f32(32, 24, 128), bf16(BLOCK, INNER), bf16(PAIRS, 256, 128)] + [f32(BLOCK, 384)] * 4
    return call(forward_kernel, args, outs, "forward", [pltpu.VMEM((4, BLOCK, 384), F32)])


def backward_kernel(
    got_ref, q_ref, k_ref, v_ref, g_ref, den_ref, w_ref, ds_ref, out_ref, dkv_ref
):
    me = time_index()
    dnorms = jnp.zeros((8, 128), F32)
    for t in range(32):
        dnorms = dnorms + jnp.where(t > me, got_ref[t, 16:24, :], 0.0)
    for p in range(PAIRS):
        lanes = slice(128 * p, 128 * p + 128)
        block, part = p // 3, slice(128 * (p % 3), 128 * (p % 3) + 128)
        fq = features(q_ref[:, lanes].astype(F32)).astype(BF16)
        k = k_ref[:, lanes].astype(F32)
        fk = features(k).astype(BF16)
        v = v_ref[:, lanes]
        dnum = (g_ref[:, lanes].astype(F32) * (1.0 / den_ref[:, lanes])).astype(BF16)
        dstate = block_diagonal(got_ref[4 * p : 4 * p + 4, 0:16, :].reshape(64, 128).astype(BF16))
        dfk = (
            mm_at(ds_ref[p], jnp.concatenate(split_pair(fq), axis=0))
            + mm_bt(v, dstate)
            + dnorms[p : p + 1, :]
        )
        dk = (dfk * slope(k)).astype(BF16)
        w = jnp.concatenate([w_ref[p, :, 0:128], w_ref[p, :, 128:256]], axis=0)
        dv = (mm_at(w, jnp.concatenate(split_pair(dnum), axis=0)) + mm(fk, dstate)).astype(BF16)
        out_ref[block, :, part] = dk.astype(F32)
        out_ref[2 + block, :, part] = dv.astype(F32)
        dkv_ref[:, lanes] = dk
        dkv_ref[:, slice(INNER + 128 * p, INNER + 128 * p + 128)] = dv


def backward(*args):
    return call(backward_kernel, args, [f32(4, BLOCK, 384), bf16(BLOCK, 2 * INNER)], "backward")


def stage_kernel(xdy_ref, x_ref, chosen_ref):
    y = lax.axis_index("y")
    sources = [lax.rem(y + 4 - i, 4) for i in range(4)]
    for j in range(8):
        lanes = slice(128 * j, 128 * j + 128)
        x = jnp.concatenate([xdy_ref[i, 0, :, lanes] for i in sources], axis=0)
        dy = jnp.concatenate([xdy_ref[i, 1, :, lanes] for i in sources], axis=0)
        x_ref[lanes, :] = x.T.astype(BF16)
        chosen_ref[lanes, :] = jnp.where(y < 2, x, dy).T.astype(BF16)


def weights_kernel(x_ref, chosen_ref, b0_ref, b1_ref, b2_ref, b3_ref, got_ref, keep_ref, give_ref):
    y, c = lax.axis_index("y"), lax.axis_index("c")
    first = [b0_ref[...], b1_ref[...], b2_ref[...], b3_ref[...]]
    second = [got_ref[lax.rem(y + s, 4)] for s in (0, 3, 2, 1)]
    for frames_ref, blocks, lanes in (
        (chosen_ref, first, slice(0, 384)),
        (x_ref, second, slice(384, 768)),
    ):
        blocks = jnp.concatenate(blocks, axis=0).astype(BF16)
        for j in range(4):
            part = mm(frames_ref[256 * j : 256 * j + 256, :], blocks).reshape(2, 4, 2, 16, 384)
            for i in range(4):
                one, two = part[:, i, 0], part[:, i, 1]
                keep_ref[i, 2 * j : 2 * j + 2, :, lanes] = jnp.where(c == 0, one, two)
                give_ref[i, 2 * j : 2 * j + 2, :, lanes] = jnp.where(c == 0, two, one)


def core_sum_kernel(keep_ref, got_ref, out_ref):
    out_ref[...] = keep_ref[...] + got_ref[...]


def row_sum_kernel(got_ref, out_ref):
    out_ref[...] = (got_ref[0] + got_ref[1]) + (got_ref[2] + got_ref[3])


def spread_kernel(got_ref, out_ref):
    total = got_ref[0]
    for i in range(1, 8):
        total = total + got_ref[i]
    for i in range(8):
        out_ref[i] = total


def frame_gradient_kernel(dq_ref, dkv_ref, w_ref, out_ref):
    for j in range(4):
        rows = slice(256 * j, 256 * j + 256)
        dx = mm_bt(dq_ref[...], w_ref[rows, 0:INNER]) + mm_bt(dkv_ref[...], w_ref[rows, INNER:])
        out_ref[:, rows] = dx.astype(BF16)


def assemble_kernel(got_ref, qkv_ref, out_ref):
    for y in range(4):
        for c in range(2):
            rows = slice(16 * c, 16 * c + 16)
            piece = got_ref[2 * y + c]
            target = qkv_ref if y < 2 else out_ref
            target[rows, 384 * (y % 2) : 384 * (y % 2) + 384] = piece[:, 0:384]
            qkv_ref[rows, INNER + 384 * y : INNER + 384 * y + 384] = piece[:, 384:768]


def swap(a, axes):
    return lax.all_to_all(a, axes, 0, 0, tiled=True)


def shift(a, axis, s):
    n = lax.axis_size(axis)
    return lax.ppermute(a, axis, [(i, (i + s) % n) for i in range(n)])


def together(*values):
    return lax.optimization_barrier(values)


def per_device(frames, grad_frames, w_qkv, w_out):
    q, k, v, g, send, xdy = project(frames[0], grad_frames[0], w_qkv, w_out)
    xdy = lax.all_gather(xdy, "y")
    send, den, norm, w = denominators(swap(send, TM), q, k, g)
    send, dq, ds, *first = forward(swap(send, TM), q, k, v, g, den, norm, w)
    first = [first[0]] + [shift(a, "y", s) for s, a in enumerate(first) if s]
    x, chosen = call(stage_kernel, (xdy,), [bf16(1024, 512)] * 2, "stage", limit=LARGE_VMEM)
    got, first, x, chosen = together(swap(send, TM), first, x, chosen)
    second, dkv = backward(got, q, k, v, g, den, w, ds)
    second = swap(second, "y")
    out = [f32(4, 8, 16, 768)] * 2
    keep, give = call(weights_kernel, (x, chosen, *first, second), out, "weights")
    (part,) = call(core_sum_kernel, (keep, shift(give, "c", 1)), out[:1], "core_sum")
    (part,) = call(row_sum_kernel, (swap(part, "x"),), [f32(8, 16, 768)], "row_sum")
    (part,) = call(spread_kernel, (swap(part, "z"),), [f32(8, 16, 768)], "spread")
    part = swap(part, DP)
    (dx,) = call(frame_gradient_kernel, (dq, dkv, w_qkv), [bf16(BLOCK, 1024)], "frame_gradient", limit=LARGE_VMEM)
    grad_qkv, grad_out = call(assemble_kernel, (part,), [f32(32, 3 * INNER), f32(32, INNER)], "assemble")
    return dx[None], grad_qkv, grad_out


def solution(mesh):
    torus = Mesh(mesh.devices.reshape(8, 4, 4, 2), TM + DP)
    rows = P(DP, TM, None)
    return jax.shard_map(
        per_device,
        mesh=torus,
        in_specs=(rows, rows, P(), P()),
        out_specs=(rows, P(TM, None), P(TM, None)),
        check_vma=False,
    )
```

```python
import jax
import jax.numpy as jnp
from jax import lax
from jax.experimental import pallas as pl
from jax.experimental.pallas import tpu as pltpu
from jax.sharding import Mesh
from jax.sharding import PartitionSpec as P

HEADS = 12
HEAD = 64
BLOCK = 128
PAIRS = HEADS // 2
INNER = HEADS * HEAD
TM = ("z", "x")
DP = ("y", "c")
F32 = jnp.float32
BF16 = jnp.bfloat16
VMEM_LIMIT = 32 * 1024 * 1024
LARGE_VMEM = 54300 * 1024
KEYS_VMEM = 54600 * 1024


def features(a):
    return jnp.where(a > 0, a + 1.0, jnp.exp(jnp.minimum(a, 0.0)))


def slope(a):
    return jnp.where(a > 0, 1.0, jnp.exp(jnp.minimum(a, 0.0)))


def low_lanes(shape):
    return lax.broadcasted_iota(jnp.int32, shape, len(shape) - 1) < HEAD


def split_pair(a):
    low = low_lanes(a.shape)
    zero = jnp.zeros_like(a)
    return jnp.where(low, a, zero), jnp.where(low, zero, a)


def block_diagonal(packed):
    first, second = split_pair(packed)
    return jnp.concatenate([first, second], axis=0)


def diagonal_blocks(m):
    return jnp.where(low_lanes((HEAD, 2 * HEAD)), m[:HEAD], m[HEAD:])


def mm(a, b):
    return lax.dot_general(a, b, (((1,), (0,)), ((), ())), preferred_element_type=F32)


def mm_bt(a, b):
    return lax.dot_general(a, b, (((1,), (1,)), ((), ())), preferred_element_type=F32)


def mm_at(a, b):
    return lax.dot_general(a, b, (((0,), (0,)), ((), ())), preferred_element_type=F32)


def causal():
    rows = lax.broadcasted_iota(jnp.int32, (BLOCK, BLOCK), 0)
    columns = lax.broadcasted_iota(jnp.int32, (BLOCK, BLOCK), 1)
    return columns <= rows


def in_vmem(n):
    return [pl.BlockSpec(memory_space=pltpu.VMEM)] * n


def in_hbm(n):
    return [pl.BlockSpec(memory_space=pltpu.HBM)] * n


def f32(*shape):
    return jax.ShapeDtypeStruct(shape, F32)


def bf16(*shape):
    return jax.ShapeDtypeStruct(shape, BF16)


def call(kernel, args, outs, name, scratch=(), in_specs=None, limit=VMEM_LIMIT):
    return pl.pallas_call(
        kernel,
        in_specs=in_specs or in_vmem(len(args)),
        out_specs=in_vmem(len(outs)),
        out_shape=outs,
        scratch_shapes=list(scratch),
        compiler_params=pltpu.CompilerParams(vmem_limit_bytes=limit),
        name=name,
    )(*args)


def time_index():
    return lax.axis_index("z") * 4 + lax.axis_index("x")


def keys_kernel(
    x_hbm, dy_hbm, w_hbm, k_ref, v_ref, send_ref, xdy_ref, x_ref, dy_ref, w_ref, sum_ref, frame_sem, weight_sem
):
    x_copy = pltpu.make_async_copy(x_hbm, x_ref, frame_sem.at[0])
    dy_copy = pltpu.make_async_copy(dy_hbm, dy_ref, frame_sem.at[1])
    x_copy.start()
    copies = []
    for i in range(4):
        rows = pl.ds(256 * i, 256)
        source = w_hbm.at[rows, pl.ds(INNER, 2 * INNER)]
        copies.append(pltpu.make_async_copy(source, w_ref.at[rows], weight_sem.at[i]))
        copies[-1].start()
    dy_copy.start()
    send_ref[24:32, 0:16, :] = jnp.zeros((8, 16, 128), F32)
    x_copy.wait()
    x = x_ref[...]
    xdy_ref[0] = x.astype(F32)
    for i in range(4):
        rows = slice(256 * i, 256 * i + 256)
        copies[i].wait()
        part = mm(x[:, rows], w_ref[rows, :])
        sum_ref[...] = part if i == 0 else sum_ref[...] + part
    norms = []
    for p in range(PAIRS):
        lanes = slice(128 * p, 128 * p + 128)
        k = sum_ref[:, lanes].astype(BF16)
        v = sum_ref[:, slice(INNER + 128 * p, INNER + 128 * p + 128)].astype(BF16)
        k_ref[:, lanes] = k
        v_ref[:, lanes] = v
        fk = features(k.astype(F32)).astype(BF16)
        state = diagonal_blocks(mm_at(fk, v))
        send_ref[4 * p : 4 * p + 4, 0:16, :] = state.reshape(4, 16, 128)
        norms.append(jnp.sum(fk.astype(F32), axis=0, keepdims=True))
    norm = jnp.concatenate(norms + [jnp.zeros((2, 128), F32)], axis=0)
    for t in range(32):
        send_ref[t, 16:24, :] = norm
    dy_copy.wait()
    xdy_ref[1] = dy_ref[...].astype(F32)


def keys(x, dy, w_qkv):
    rows, width = x.shape
    scratch = [pltpu.VMEM((rows, width), BF16)] * 2 + [pltpu.VMEM((width, 2 * INNER), BF16)]
    scratch += [pltpu.VMEM((rows, 2 * INNER), F32)]
    scratch += [pltpu.SemaphoreType.DMA((2,)), pltpu.SemaphoreType.DMA((4,))]
    outs = [bf16(rows, INNER)] * 2 + [f32(32, 24, 128), f32(2, rows, width)]
    return call(keys_kernel, (x, dy, w_qkv), outs, "keys", scratch, in_hbm(3), KEYS_VMEM)


def queries_kernel(
    x_hbm, dy_hbm, w_hbm, wo_hbm, k_ref, q_ref, g_ref, w_ref, sums_ref,
    x_ref, dy_ref, wq_ref, wo_ref, sems,
):
    copies = [
        pltpu.make_async_copy(x_hbm, x_ref, sems.at[0]),
        pltpu.make_async_copy(w_hbm.at[:, pl.ds(0, INNER)], wq_ref, sems.at[1]),
        pltpu.make_async_copy(dy_hbm, dy_ref, sems.at[2]),
        pltpu.make_async_copy(wo_hbm, wo_ref, sems.at[3]),
    ]
    for copy in copies:
        copy.start()
    copies[0].wait()
    copies[1].wait()
    mask = causal()
    lane = lax.broadcasted_iota(jnp.int32, (BLOCK, 128), 1)
    packed = jnp.zeros((BLOCK, 128), F32)
    for step in range(3):
        wide = slice(256 * step, 256 * step + 256)
        q_ref[:, wide] = mm(x_ref[...], wq_ref[:, wide]).astype(BF16)
        for p in (2 * step, 2 * step + 1):
            lanes = slice(128 * p, 128 * p + 128)
            fq = features(q_ref[:, lanes].astype(F32)).astype(BF16)
            fk = features(k_ref[:, lanes].astype(F32)).astype(BF16)
            for half, rows in enumerate(split_pair(fq)):
                scores = jnp.where(mask, mm_bt(rows, fk), 0.0)
                w_ref[p, :, 128 * half : 128 * half + 128] = scores.astype(BF16)
                packed = jnp.where(lane == 2 * p + half, jnp.sum(scores, axis=1, keepdims=True), packed)
    sums_ref[...] = packed
    copies[2].wait()
    copies[3].wait()
    for step in range(3):
        wide = slice(256 * step, 256 * step + 256)
        g_ref[:, wide] = mm(dy_ref[...], wo_ref[:, wide]).astype(BF16)


def queries(x, dy, w_qkv, w_out, k):
    rows, width = x.shape
    scratch = [pltpu.VMEM((rows, width), BF16)] * 2 + [pltpu.VMEM((width, INNER), BF16)] * 2
    scratch += [pltpu.SemaphoreType.DMA((4,))]
    outs = [bf16(rows, INNER)] * 2 + [bf16(PAIRS, BLOCK, 256), f32(BLOCK, 128)]
    specs = in_hbm(4) + in_vmem(1)
    return call(queries_kernel, (x, dy, w_qkv, w_out, k), outs, "queries", scratch, specs, LARGE_VMEM)


def denominators_kernel(got_ref, q_ref, g_ref, sums_ref, send_ref, inverse_ref, dnum_ref, norm_ref):
    me = time_index()
    carry = jnp.zeros((16, 128), F32)
    norms = jnp.zeros((8, 128), F32)
    for t in range(32):
        send_ref[t, 0:16, :] = carry
        carry = carry + got_ref[t, 0:16, :]
        norms = norms + jnp.where(t < me, got_ref[t, 16:24, :], 0.0)
    norm_ref[...] = norms
    lane = lax.broadcasted_iota(jnp.int32, (BLOCK, 128), 1)
    packed = jnp.ones((BLOCK, 128), F32)
    for p in range(PAIRS):
        lanes = slice(128 * p, 128 * p + 128)
        fq = features(q_ref[:, lanes].astype(F32)).astype(BF16)
        dots = [
            jnp.sum(a, axis=1, keepdims=True) + sums_ref[:, 2 * p + half : 2 * p + half + 1]
            for half, a in enumerate(split_pair(fq.astype(F32) * norms[p : p + 1, :]))
        ]
        for half in range(2):
            packed = jnp.where(lane == 2 * p + half, dots[half], packed)
        den = jnp.where(low_lanes((BLOCK, 128)), dots[0], dots[1])
        dnum = (g_ref[:, lanes].astype(F32) / den).astype(BF16)
        dnum_ref[:, lanes] = dnum
        dstate = diagonal_blocks(mm_at(fq, dnum))
        send_ref[4 * p : 4 * p + 4, 16:32, :] = dstate.reshape(4, 16, 128)
    inverse_ref[...] = 1.0 / packed
    send_ref[24:32, 16:32, :] = jnp.zeros((8, 16, 128), F32)


def denominators(*args):
    outs = [f32(32, 32, 128), f32(BLOCK, 128), bf16(BLOCK, INNER), f32(8, 128)]
    return call(denominators_kernel, args, outs, "denominators")


def forward_kernel(
    got_ref, q_ref, k_ref, v_ref, g_ref, inverse_ref, dnum_ref, norm_ref, w_ref,
    send_ref, dq_ref, ds_ref, b0_ref, b1_ref, b2_ref, b3_ref, out_ref,
):
    carry = jnp.zeros((16, 128), F32)
    for t in reversed(range(32)):
        send_ref[t, 0:16, :] = carry
        carry = carry + got_ref[t, 16:32, :]
    mask = causal()
    low = low_lanes((BLOCK, 128))
    dnorms = []
    for p in range(PAIRS):
        lanes = slice(128 * p, 128 * p + 128)
        block, part = p // 3, slice(128 * (p % 3), 128 * (p % 3) + 128)
        q = q_ref[:, lanes].astype(F32)
        fq = features(q).astype(BF16)
        fk = features(k_ref[:, lanes].astype(F32)).astype(BF16)
        v = v_ref[:, lanes]
        g = g_ref[:, lanes].astype(F32)
        inverse = jnp.where(
            low, inverse_ref[:, 2 * p : 2 * p + 1], inverse_ref[:, 2 * p + 1 : 2 * p + 2]
        )
        state = block_diagonal(got_ref[4 * p : 4 * p + 4, 0:16, :].reshape(64, 128).astype(BF16))
        v_halves = jnp.concatenate(split_pair(v), axis=0)
        ratio = (mm(w_ref[p], v_halves) + mm(fq, state)) * inverse
        out_ref[2 + block, :, part] = ratio.astype(BF16).astype(F32)
        dnum = dnum_ref[:, lanes]
        sums = [jnp.sum(a, axis=1, keepdims=True) for a in split_pair(g * ratio)]
        dden = -jnp.where(low, sums[0], sums[1]) * inverse
        ddens = (dden[:, 0:1], dden[:, 127:128])
        dnorms.append(jnp.sum(dden * fq.astype(F32), axis=0, keepdims=True))
        ds = [
            jnp.where(mask, mm_bt(rows, v) + column, 0.0).astype(BF16)
            for rows, column in zip(split_pair(dnum), ddens)
        ]
        ds_ref[p] = jnp.concatenate(ds, axis=0)
        dfq = (
            mm(jnp.concatenate(ds, axis=1), jnp.concatenate(split_pair(fk), axis=0))
            + mm_bt(dnum, state)
            + dden * norm_ref[p : p + 1, :]
        )
        dq = (dfq * slope(q)).astype(BF16)
        dq_ref[:, lanes] = dq
        out_ref[block, :, part] = dq.astype(F32)
    dnorm = jnp.concatenate(dnorms + [jnp.zeros((2, 128), F32)], axis=0)
    for t in range(32):
        send_ref[t, 16:24, :] = dnorm
    y = lax.axis_index("y")
    for i, ref in enumerate((b0_ref, b1_ref, b2_ref, b3_ref)):
        ref[...] = out_ref[lax.rem(y + i, 4)]


def forward(*args):
    outs = [f32(32, 24, 128), bf16(BLOCK, INNER), bf16(PAIRS, 256, 128)] + [f32(BLOCK, 384)] * 4
    return call(forward_kernel, args, outs, "forward", [pltpu.VMEM((4, BLOCK, 384), F32)])


def backward_kernel(
    got_ref, q_ref, k_ref, v_ref, dnum_ref, w_ref, ds_ref, out_ref, dkv_ref
):
    me = time_index()
    dnorms = jnp.zeros((8, 128), F32)
    for t in range(32):
        dnorms = dnorms + jnp.where(t > me, got_ref[t, 16:24, :], 0.0)
    for p in range(PAIRS):
        lanes = slice(128 * p, 128 * p + 128)
        block, part = p // 3, slice(128 * (p % 3), 128 * (p % 3) + 128)
        fq = features(q_ref[:, lanes].astype(F32)).astype(BF16)
        k = k_ref[:, lanes].astype(F32)
        fk = features(k).astype(BF16)
        v = v_ref[:, lanes]
        dnum = dnum_ref[:, lanes]
        dstate = block_diagonal(got_ref[4 * p : 4 * p + 4, 0:16, :].reshape(64, 128).astype(BF16))
        dfk = (
            mm_at(ds_ref[p], jnp.concatenate(split_pair(fq), axis=0))
            + mm_bt(v, dstate)
            + dnorms[p : p + 1, :]
        )
        dk = (dfk * slope(k)).astype(BF16)
        w = jnp.concatenate([w_ref[p, :, 0:128], w_ref[p, :, 128:256]], axis=0)
        dv = (mm_at(w, jnp.concatenate(split_pair(dnum), axis=0)) + mm(fk, dstate)).astype(BF16)
        out_ref[block, :, part] = dk.astype(F32)
        out_ref[2 + block, :, part] = dv.astype(F32)
        dkv_ref[:, lanes] = dk
        dkv_ref[:, slice(INNER + 128 * p, INNER + 128 * p + 128)] = dv


def backward(*args):
    return call(backward_kernel, args, [f32(4, BLOCK, 384), bf16(BLOCK, 2 * INNER)], "backward")


def stage_kernel(xdy_ref, x_ref, chosen_ref):
    y = lax.axis_index("y")
    sources = [lax.rem(y + 4 - i, 4) for i in range(4)]
    for j in range(8):
        lanes = slice(128 * j, 128 * j + 128)
        x = jnp.concatenate([xdy_ref[i, 0, :, lanes] for i in sources], axis=0)
        dy = jnp.concatenate([xdy_ref[i, 1, :, lanes] for i in sources], axis=0)
        x_ref[lanes, :] = x.T.astype(BF16)
        chosen_ref[lanes, :] = jnp.where(y < 2, x, dy).T.astype(BF16)


def weights_kernel(x_ref, chosen_ref, b0_ref, b1_ref, b2_ref, b3_ref, got_ref, keep_ref, give_ref):
    y, c = lax.axis_index("y"), lax.axis_index("c")
    first = [b0_ref[...], b1_ref[...], b2_ref[...], b3_ref[...]]
    second = [got_ref[lax.rem(y + s, 4)] for s in (0, 3, 2, 1)]
    for frames_ref, blocks, lanes in (
        (chosen_ref, first, slice(0, 384)),
        (x_ref, second, slice(384, 768)),
    ):
        blocks = jnp.concatenate(blocks, axis=0).astype(BF16)
        for j in range(4):
            part = mm(frames_ref[256 * j : 256 * j + 256, :], blocks).reshape(2, 4, 2, 16, 384)
            for i in range(4):
                one, two = part[:, i, 0], part[:, i, 1]
                keep_ref[i, 2 * j : 2 * j + 2, :, lanes] = jnp.where(c == 0, one, two)
                give_ref[i, 2 * j : 2 * j + 2, :, lanes] = jnp.where(c == 0, two, one)


def core_sum_kernel(keep_ref, got_ref, out_ref):
    out_ref[...] = keep_ref[...] + got_ref[...]


def row_sum_kernel(got_ref, out_ref):
    out_ref[...] = (got_ref[0] + got_ref[1]) + (got_ref[2] + got_ref[3])


def spread_kernel(got_ref, out_ref):
    total = got_ref[0]
    for i in range(1, 8):
        total = total + got_ref[i]
    for i in range(8):
        out_ref[i] = total


def frame_gradient_kernel(dq_ref, dkv_ref, w_ref, out_ref):
    for j in range(4):
        rows = slice(256 * j, 256 * j + 256)
        dx = mm_bt(dq_ref[...], w_ref[rows, 0:INNER]) + mm_bt(dkv_ref[...], w_ref[rows, INNER:])
        out_ref[:, rows] = dx.astype(BF16)


def assemble_kernel(got_ref, qkv_ref, out_ref):
    for y in range(4):
        for c in range(2):
            rows = slice(16 * c, 16 * c + 16)
            piece = got_ref[2 * y + c]
            target = qkv_ref if y < 2 else out_ref
            target[rows, 384 * (y % 2) : 384 * (y % 2) + 384] = piece[:, 0:384]
            qkv_ref[rows, INNER + 384 * y : INNER + 384 * y + 384] = piece[:, 384:768]


def swap(a, axes):
    return lax.all_to_all(a, axes, 0, 0, tiled=True)


def shift(a, axis, s):
    n = lax.axis_size(axis)
    return lax.ppermute(a, axis, [(i, (i + s) % n) for i in range(n)])


def together(*values):
    return lax.optimization_barrier(values)


def per_device(frames, grad_frames, w_qkv, w_out):
    k, v, send, xdy = keys(frames[0], grad_frames[0], w_qkv)
    xdy = lax.all_gather(xdy, "y")
    q, g, w, sums = queries(frames[0], grad_frames[0], w_qkv, w_out, k)
    got, q, g, w, sums = together(swap(send, TM), q, g, w, sums)
    send, inverse, dnum, norm = denominators(got, q, g, sums)
    send, dq, ds, *first = forward(swap(send, TM), q, k, v, g, inverse, dnum, norm, w)
    first = [first[0]] + [shift(a, "y", s) for s, a in enumerate(first) if s]
    x, chosen = call(stage_kernel, (xdy,), [bf16(1024, 512)] * 2, "stage", limit=LARGE_VMEM)
    got, first, x, chosen = together(swap(send, TM), first, x, chosen)
    second, dkv = backward(got, q, k, v, dnum, w, ds)
    second = swap(second, "y")
    out = [f32(4, 8, 16, 768)] * 2
    keep, give = call(weights_kernel, (x, chosen, *first, second), out, "weights")
    (part,) = call(core_sum_kernel, (keep, shift(give, "c", 1)), out[:1], "core_sum")
    (part,) = call(row_sum_kernel, (swap(part, "x"),), [f32(8, 16, 768)], "row_sum")
    (part,) = call(spread_kernel, (swap(part, "z"),), [f32(8, 16, 768)], "spread")
    part = swap(part, DP)
    (dx,) = call(frame_gradient_kernel, (dq, dkv, w_qkv), [bf16(BLOCK, 1024)], "frame_gradient", limit=LARGE_VMEM)
    grad_qkv, grad_out = call(assemble_kernel, (part,), [f32(32, 3 * INNER), f32(32, INNER)], "assemble")
    return dx[None], grad_qkv, grad_out


def solution(mesh):
    torus = Mesh(mesh.devices.reshape(8, 4, 4, 2), TM + DP)
    rows = P(DP, TM, None)
    return jax.shard_map(
        per_device,
        mesh=torus,
        in_specs=(rows, rows, P(), P()),
        out_specs=(rows, P(TM, None), P(TM, None)),
        check_vma=False,
    )
```

```python
import jax
import jax.numpy as jnp
from jax import lax
from jax.experimental import pallas as pl
from jax.experimental.pallas import tpu as pltpu
from jax.sharding import Mesh
from jax.sharding import PartitionSpec as P

HEADS = 12
HEAD = 64
BLOCK = 128
PAIRS = HEADS // 2
INNER = HEADS * HEAD
TM = ("z", "x")
DP = ("y", "c")
F32 = jnp.float32
BF16 = jnp.bfloat16
VMEM_LIMIT = 32 * 1024 * 1024
LARGE_VMEM = 54300 * 1024
KEYS_VMEM = 54600 * 1024


def features(a):
    return jnp.where(a > 0, a + 1.0, jnp.exp(jnp.minimum(a, 0.0)))


def slope(a):
    return jnp.where(a > 0, 1.0, jnp.exp(jnp.minimum(a, 0.0)))


def low_lanes(shape):
    return lax.broadcasted_iota(jnp.int32, shape, len(shape) - 1) < HEAD


def split_pair(a):
    low = low_lanes(a.shape)
    zero = jnp.zeros_like(a)
    return jnp.where(low, a, zero), jnp.where(low, zero, a)


def block_diagonal(packed):
    first, second = split_pair(packed)
    return jnp.concatenate([first, second], axis=0)


def diagonal_blocks(m):
    return jnp.where(low_lanes((HEAD, 2 * HEAD)), m[:HEAD], m[HEAD:])


def mm(a, b):
    return lax.dot_general(a, b, (((1,), (0,)), ((), ())), preferred_element_type=F32)


def mm_bt(a, b):
    return lax.dot_general(a, b, (((1,), (1,)), ((), ())), preferred_element_type=F32)


def mm_at(a, b):
    return lax.dot_general(a, b, (((0,), (0,)), ((), ())), preferred_element_type=F32)


def causal():
    rows = lax.broadcasted_iota(jnp.int32, (BLOCK, BLOCK), 0)
    columns = lax.broadcasted_iota(jnp.int32, (BLOCK, BLOCK), 1)
    return columns <= rows


def in_vmem(n):
    return [pl.BlockSpec(memory_space=pltpu.VMEM)] * n


def in_hbm(n):
    return [pl.BlockSpec(memory_space=pltpu.HBM)] * n


def f32(*shape):
    return jax.ShapeDtypeStruct(shape, F32)


def bf16(*shape):
    return jax.ShapeDtypeStruct(shape, BF16)


def call(kernel, args, outs, name, scratch=(), in_specs=None, limit=VMEM_LIMIT):
    return pl.pallas_call(
        kernel,
        in_specs=in_specs or in_vmem(len(args)),
        out_specs=in_vmem(len(outs)),
        out_shape=outs,
        scratch_shapes=list(scratch),
        compiler_params=pltpu.CompilerParams(vmem_limit_bytes=limit),
        name=name,
    )(*args)


def scatter_rows(state_ref, send_ref, first):
    for t in range(32):
        send_ref[t, first : first + 12, :] = state_ref[12 * t : 12 * t + 12, :]


def gather_rows(got_ref, state_ref):
    for t in range(32):
        state_ref[12 * t : 12 * t + 12, :] = got_ref[t, 0:12, :]


STATE = pltpu.VMEM((384, 128), F32)


def time_index():
    return lax.axis_index("z") * 4 + lax.axis_index("x")


def keys_kernel(
    x_hbm, dy_hbm, w_hbm, k_ref, v_ref, send_ref, xdy_ref, x_ref, dy_ref, w_ref, sum_ref, state_ref, frame_sem, weight_sem
):
    x_copy = pltpu.make_async_copy(x_hbm, x_ref, frame_sem.at[0])
    dy_copy = pltpu.make_async_copy(dy_hbm, dy_ref, frame_sem.at[1])
    x_copy.start()
    copies = []
    for i in range(4):
        rows = pl.ds(256 * i, 256)
        source = w_hbm.at[rows, pl.ds(INNER, 2 * INNER)]
        copies.append(pltpu.make_async_copy(source, w_ref.at[rows], weight_sem.at[i]))
        copies[-1].start()
    dy_copy.start()
    x_copy.wait()
    x = x_ref[...]
    xdy_ref[0] = x.astype(F32)
    for i in range(4):
        rows = slice(256 * i, 256 * i + 256)
        copies[i].wait()
        part = mm(x[:, rows], w_ref[rows, :])
        sum_ref[...] = part if i == 0 else sum_ref[...] + part
    norms = []
    for p in range(PAIRS):
        lanes = slice(128 * p, 128 * p + 128)
        k = sum_ref[:, lanes].astype(BF16)
        v = sum_ref[:, slice(INNER + 128 * p, INNER + 128 * p + 128)].astype(BF16)
        k_ref[:, lanes] = k
        v_ref[:, lanes] = v
        fk = features(k.astype(F32)).astype(BF16)
        state = diagonal_blocks(mm_at(fk, v))
        state_ref[64 * p : 64 * p + 64, :] = state
        norms.append(jnp.sum(fk.astype(F32), axis=0, keepdims=True))
    scatter_rows(state_ref, send_ref, 0)
    norm = jnp.concatenate(norms + [jnp.zeros((6, 128), F32)], axis=0)
    for t in range(32):
        send_ref[t, 12:24, :] = norm
    dy_copy.wait()
    xdy_ref[1] = dy_ref[...].astype(F32)


def keys(x, dy, w_qkv):
    rows, width = x.shape
    scratch = [pltpu.VMEM((rows, width), BF16)] * 2 + [pltpu.VMEM((width, 2 * INNER), BF16)]
    scratch += [pltpu.VMEM((rows, 2 * INNER), F32), STATE]
    scratch += [pltpu.SemaphoreType.DMA((2,)), pltpu.SemaphoreType.DMA((4,))]
    outs = [bf16(rows, INNER)] * 2 + [f32(32, 24, 128), f32(2, rows, width)]
    return call(keys_kernel, (x, dy, w_qkv), outs, "keys", scratch, in_hbm(3), KEYS_VMEM)


def queries_kernel(
    x_hbm, dy_hbm, w_hbm, wo_hbm, k_ref, q_ref, g_ref, w_ref, sums_ref,
    x_ref, dy_ref, wq_ref, wo_ref, sems,
):
    copies = [
        pltpu.make_async_copy(x_hbm, x_ref, sems.at[0]),
        pltpu.make_async_copy(w_hbm.at[:, pl.ds(0, INNER)], wq_ref, sems.at[1]),
        pltpu.make_async_copy(dy_hbm, dy_ref, sems.at[2]),
        pltpu.make_async_copy(wo_hbm, wo_ref, sems.at[3]),
    ]
    for copy in copies:
        copy.start()
    copies[0].wait()
    copies[1].wait()
    mask = causal()
    lane = lax.broadcasted_iota(jnp.int32, (BLOCK, 128), 1)
    packed = jnp.zeros((BLOCK, 128), F32)
    for step in range(3):
        wide = slice(256 * step, 256 * step + 256)
        q_ref[:, wide] = mm(x_ref[...], wq_ref[:, wide]).astype(BF16)
        for p in (2 * step, 2 * step + 1):
            lanes = slice(128 * p, 128 * p + 128)
            fq = features(q_ref[:, lanes].astype(F32)).astype(BF16)
            fk = features(k_ref[:, lanes].astype(F32)).astype(BF16)
            for half, rows in enumerate(split_pair(fq)):
                scores = jnp.where(mask, mm_bt(rows, fk), 0.0)
                w_ref[p, :, 128 * half : 128 * half + 128] = scores.astype(BF16)
                packed = jnp.where(lane == 2 * p + half, jnp.sum(scores, axis=1, keepdims=True), packed)
    sums_ref[...] = packed
    copies[2].wait()
    copies[3].wait()
    for step in range(3):
        wide = slice(256 * step, 256 * step + 256)
        g_ref[:, wide] = mm(dy_ref[...], wo_ref[:, wide]).astype(BF16)


def queries(x, dy, w_qkv, w_out, k):
    rows, width = x.shape
    scratch = [pltpu.VMEM((rows, width), BF16)] * 2 + [pltpu.VMEM((width, INNER), BF16)] * 2
    scratch += [pltpu.SemaphoreType.DMA((4,))]
    outs = [bf16(rows, INNER)] * 2 + [bf16(PAIRS, BLOCK, 256), f32(BLOCK, 128)]
    specs = in_hbm(4) + in_vmem(1)
    return call(queries_kernel, (x, dy, w_qkv, w_out, k), outs, "queries", scratch, specs, LARGE_VMEM)


def denominators_kernel(got_ref, q_ref, g_ref, sums_ref, send_ref, inverse_ref, dnum_ref, norm_ref, state_ref):
    me = time_index()
    carry = jnp.zeros((12, 128), F32)
    norms = jnp.zeros((8, 128), F32)
    for t in range(32):
        send_ref[t, 0:12, :] = carry
        carry = carry + got_ref[t, 0:12, :]
        norms = norms + jnp.where(t < me, got_ref[t, 12:20, :], 0.0)
    norm_ref[...] = norms
    lane = lax.broadcasted_iota(jnp.int32, (BLOCK, 128), 1)
    packed = jnp.ones((BLOCK, 128), F32)
    for p in range(PAIRS):
        lanes = slice(128 * p, 128 * p + 128)
        fq = features(q_ref[:, lanes].astype(F32)).astype(BF16)
        dots = [
            jnp.sum(a, axis=1, keepdims=True) + sums_ref[:, 2 * p + half : 2 * p + half + 1]
            for half, a in enumerate(split_pair(fq.astype(F32) * norms[p : p + 1, :]))
        ]
        for half in range(2):
            packed = jnp.where(lane == 2 * p + half, dots[half], packed)
        den = jnp.where(low_lanes((BLOCK, 128)), dots[0], dots[1])
        dnum = (g_ref[:, lanes].astype(F32) / den).astype(BF16)
        dnum_ref[:, lanes] = dnum
        dstate = diagonal_blocks(mm_at(fq, dnum))
        state_ref[64 * p : 64 * p + 64, :] = dstate
    inverse_ref[...] = 1.0 / packed
    scatter_rows(state_ref, send_ref, 12)


def denominators(*args):
    outs = [f32(32, 24, 128), f32(BLOCK, 128), bf16(BLOCK, INNER), f32(8, 128)]
    return call(denominators_kernel, args, outs, "denominators", [STATE])


def forward_kernel(
    got_ref, q_ref, k_ref, v_ref, g_ref, inverse_ref, dnum_ref, norm_ref, w_ref,
    send_ref, dq_ref, ds_ref, b0_ref, b1_ref, b2_ref, b3_ref, out_ref, state_ref,
):
    gather_rows(got_ref, state_ref)
    carry = jnp.zeros((12, 128), F32)
    for t in reversed(range(32)):
        send_ref[t, 0:12, :] = carry
        carry = carry + got_ref[t, 12:24, :]
    mask = causal()
    low = low_lanes((BLOCK, 128))
    dnorms = []
    for p in range(PAIRS):
        lanes = slice(128 * p, 128 * p + 128)
        block, part = p // 3, slice(128 * (p % 3), 128 * (p % 3) + 128)
        q = q_ref[:, lanes].astype(F32)
        fq = features(q).astype(BF16)
        fk = features(k_ref[:, lanes].astype(F32)).astype(BF16)
        v = v_ref[:, lanes]
        g = g_ref[:, lanes].astype(F32)
        inverse = jnp.where(
            low, inverse_ref[:, 2 * p : 2 * p + 1], inverse_ref[:, 2 * p + 1 : 2 * p + 2]
        )
        state = block_diagonal(state_ref[64 * p : 64 * p + 64, :].astype(BF16))
        v_halves = jnp.concatenate(split_pair(v), axis=0)
        ratio = (mm(w_ref[p], v_halves) + mm(fq, state)) * inverse
        out_ref[2 + block, :, part] = ratio.astype(BF16).astype(F32)
        dnum = dnum_ref[:, lanes]
        sums = [jnp.sum(a, axis=1, keepdims=True) for a in split_pair(g * ratio)]
        dden = -jnp.where(low, sums[0], sums[1]) * inverse
        ddens = (dden[:, 0:1], dden[:, 127:128])
        dnorms.append(jnp.sum(dden * fq.astype(F32), axis=0, keepdims=True))
        ds = [
            jnp.where(mask, mm_bt(rows, v) + column, 0.0).astype(BF16)
            for rows, column in zip(split_pair(dnum), ddens)
        ]
        ds_ref[p] = jnp.concatenate(ds, axis=0)
        dfq = (
            mm(jnp.concatenate(ds, axis=1), jnp.concatenate(split_pair(fk), axis=0))
            + mm_bt(dnum, state)
            + dden * norm_ref[p : p + 1, :]
        )
        dq = (dfq * slope(q)).astype(BF16)
        dq_ref[:, lanes] = dq
        out_ref[block, :, part] = dq.astype(F32)
    dnorm = jnp.concatenate(dnorms + [jnp.zeros((6, 128), F32)], axis=0)
    for t in range(32):
        send_ref[t, 12:24, :] = dnorm
    y = lax.axis_index("y")
    for i, ref in enumerate((b0_ref, b1_ref, b2_ref, b3_ref)):
        ref[...] = out_ref[lax.rem(y + i, 4)]


def forward(*args):
    outs = [f32(32, 24, 128), bf16(BLOCK, INNER), bf16(PAIRS, 256, 128)] + [f32(BLOCK, 384)] * 4
    return call(forward_kernel, args, outs, "forward", [pltpu.VMEM((4, BLOCK, 384), F32), STATE])


def backward_kernel(
    got_ref, q_ref, k_ref, v_ref, dnum_ref, w_ref, ds_ref, out_ref, dkv_ref, state_ref
):
    me = time_index()
    dnorms = jnp.zeros((8, 128), F32)
    for t in range(32):
        dnorms = dnorms + jnp.where(t > me, got_ref[t, 12:20, :], 0.0)
    gather_rows(got_ref, state_ref)
    for p in range(PAIRS):
        lanes = slice(128 * p, 128 * p + 128)
        block, part = p // 3, slice(128 * (p % 3), 128 * (p % 3) + 128)
        fq = features(q_ref[:, lanes].astype(F32)).astype(BF16)
        k = k_ref[:, lanes].astype(F32)
        fk = features(k).astype(BF16)
        v = v_ref[:, lanes]
        dnum = dnum_ref[:, lanes]
        dstate = block_diagonal(state_ref[64 * p : 64 * p + 64, :].astype(BF16))
        dfk = (
            mm_at(ds_ref[p], jnp.concatenate(split_pair(fq), axis=0))
            + mm_bt(v, dstate)
            + dnorms[p : p + 1, :]
        )
        dk = (dfk * slope(k)).astype(BF16)
        w = jnp.concatenate([w_ref[p, :, 0:128], w_ref[p, :, 128:256]], axis=0)
        dv = (mm_at(w, jnp.concatenate(split_pair(dnum), axis=0)) + mm(fk, dstate)).astype(BF16)
        out_ref[block, :, part] = dk.astype(F32)
        out_ref[2 + block, :, part] = dv.astype(F32)
        dkv_ref[:, lanes] = dk
        dkv_ref[:, slice(INNER + 128 * p, INNER + 128 * p + 128)] = dv


def backward(*args):
    return call(backward_kernel, args, [f32(4, BLOCK, 384), bf16(BLOCK, 2 * INNER)], "backward", [STATE])


def stage_kernel(xdy_ref, x_ref, chosen_ref):
    y = lax.axis_index("y")
    sources = [lax.rem(y + 4 - i, 4) for i in range(4)]
    for j in range(8):
        lanes = slice(128 * j, 128 * j + 128)
        x = jnp.concatenate([xdy_ref[i, 0, :, lanes] for i in sources], axis=0)
        dy = jnp.concatenate([xdy_ref[i, 1, :, lanes] for i in sources], axis=0)
        x_ref[lanes, :] = x.T.astype(BF16)
        chosen_ref[lanes, :] = jnp.where(y < 2, x, dy).T.astype(BF16)


def weights_kernel(x_ref, chosen_ref, b0_ref, b1_ref, b2_ref, b3_ref, got_ref, keep_ref, give_ref):
    y, c = lax.axis_index("y"), lax.axis_index("c")
    first = [b0_ref[...], b1_ref[...], b2_ref[...], b3_ref[...]]
    second = [got_ref[lax.rem(y + s, 4)] for s in (0, 3, 2, 1)]
    for frames_ref, blocks, lanes in (
        (chosen_ref, first, slice(0, 384)),
        (x_ref, second, slice(384, 768)),
    ):
        blocks = jnp.concatenate(blocks, axis=0).astype(BF16)
        for j in range(4):
            part = mm(frames_ref[256 * j : 256 * j + 256, :], blocks).reshape(2, 4, 2, 16, 384)
            for i in range(4):
                one, two = part[:, i, 0], part[:, i, 1]
                keep_ref[i, 2 * j : 2 * j + 2, :, lanes] = jnp.where(c == 0, one, two)
                give_ref[i, 2 * j : 2 * j + 2, :, lanes] = jnp.where(c == 0, two, one)


def core_sum_kernel(keep_ref, got_ref, out_ref):
    out_ref[...] = keep_ref[...] + got_ref[...]


def row_sum_kernel(got_ref, out_ref):
    out_ref[...] = (got_ref[0] + got_ref[1]) + (got_ref[2] + got_ref[3])


def spread_kernel(got_ref, out_ref):
    total = got_ref[0]
    for i in range(1, 8):
        total = total + got_ref[i]
    for i in range(8):
        out_ref[i] = total


def frame_gradient_kernel(dq_ref, dkv_ref, w_ref, out_ref):
    for j in range(4):
        rows = slice(256 * j, 256 * j + 256)
        dx = mm_bt(dq_ref[...], w_ref[rows, 0:INNER]) + mm_bt(dkv_ref[...], w_ref[rows, INNER:])
        out_ref[:, rows] = dx.astype(BF16)


def assemble_kernel(got_ref, qkv_ref, out_ref):
    for y in range(4):
        for c in range(2):
            rows = slice(16 * c, 16 * c + 16)
            piece = got_ref[2 * y + c]
            target = qkv_ref if y < 2 else out_ref
            target[rows, 384 * (y % 2) : 384 * (y % 2) + 384] = piece[:, 0:384]
            qkv_ref[rows, INNER + 384 * y : INNER + 384 * y + 384] = piece[:, 384:768]


def swap(a, axes):
    return lax.all_to_all(a, axes, 0, 0, tiled=True)


def shift(a, axis, s):
    n = lax.axis_size(axis)
    return lax.ppermute(a, axis, [(i, (i + s) % n) for i in range(n)])


def together(*values):
    return lax.optimization_barrier(values)


def per_device(frames, grad_frames, w_qkv, w_out):
    k, v, send, xdy = keys(frames[0], grad_frames[0], w_qkv)
    xdy = lax.all_gather(xdy, "y")
    q, g, w, sums = queries(frames[0], grad_frames[0], w_qkv, w_out, k)
    got, q, g, w, sums = together(swap(send, TM), q, g, w, sums)
    send, inverse, dnum, norm = denominators(got, q, g, sums)
    send, dq, ds, *first = forward(swap(send, TM), q, k, v, g, inverse, dnum, norm, w)
    first = [first[0]] + [shift(a, "y", s) for s, a in enumerate(first) if s]
    x, chosen = call(stage_kernel, (xdy,), [bf16(1024, 512)] * 2, "stage", limit=LARGE_VMEM)
    got, first, x, chosen = together(swap(send, TM), first, x, chosen)
    second, dkv = backward(got, q, k, v, dnum, w, ds)
    second = swap(second, "y")
    out = [f32(4, 8, 16, 768)] * 2
    keep, give = call(weights_kernel, (x, chosen, *first, second), out, "weights")
    (part,) = call(core_sum_kernel, (keep, shift(give, "c", 1)), out[:1], "core_sum")
    (part,) = call(row_sum_kernel, (swap(part, "x"),), [f32(8, 16, 768)], "row_sum")
    (part,) = call(spread_kernel, (swap(part, "z"),), [f32(8, 16, 768)], "spread")
    part = swap(part, DP)
    (dx,) = call(frame_gradient_kernel, (dq, dkv, w_qkv), [bf16(BLOCK, 1024)], "frame_gradient", limit=LARGE_VMEM)
    grad_qkv, grad_out = call(assemble_kernel, (part,), [f32(32, 3 * INNER), f32(32, INNER)], "assemble")
    return dx[None], grad_qkv, grad_out


def solution(mesh):
    torus = Mesh(mesh.devices.reshape(8, 4, 4, 2), TM + DP)
    rows = P(DP, TM, None)
    return jax.shard_map(
        per_device,
        mesh=torus,
        in_specs=(rows, rows, P(), P()),
        out_specs=(rows, P(TM, None), P(TM, None)),
        check_vma=False,
    )
```

```python
import jax
import jax.numpy as jnp
from jax import lax
from jax.experimental import pallas as pl
from jax.experimental.pallas import tpu as pltpu
from jax.sharding import Mesh
from jax.sharding import PartitionSpec as P

HEADS = 12
HEAD = 64
BLOCK = 128
PAIRS = HEADS // 2
INNER = HEADS * HEAD
TM = ("z", "x")
DP = ("y", "c")
F32 = jnp.float32
BF16 = jnp.bfloat16
VMEM_LIMIT = 32 * 1024 * 1024
LARGE_VMEM = 54300 * 1024
KEYS_VMEM = 54600 * 1024


def features(a):
    return jnp.where(a > 0, a + 1.0, jnp.exp(jnp.minimum(a, 0.0)))


def slope(a):
    return jnp.where(a > 0, 1.0, jnp.exp(jnp.minimum(a, 0.0)))


def low_lanes(shape):
    return lax.broadcasted_iota(jnp.int32, shape, len(shape) - 1) < HEAD


def split_pair(a):
    low = low_lanes(a.shape)
    zero = jnp.zeros_like(a)
    return jnp.where(low, a, zero), jnp.where(low, zero, a)


def block_diagonal(packed):
    first, second = split_pair(packed)
    return jnp.concatenate([first, second], axis=0)


def diagonal_blocks(m):
    return jnp.where(low_lanes((HEAD, 2 * HEAD)), m[:HEAD], m[HEAD:])


def mm(a, b):
    return lax.dot_general(a, b, (((1,), (0,)), ((), ())), preferred_element_type=F32)


def mm_bt(a, b):
    return lax.dot_general(a, b, (((1,), (1,)), ((), ())), preferred_element_type=F32)


def mm_at(a, b):
    return lax.dot_general(a, b, (((0,), (0,)), ((), ())), preferred_element_type=F32)


def causal():
    rows = lax.broadcasted_iota(jnp.int32, (BLOCK, BLOCK), 0)
    columns = lax.broadcasted_iota(jnp.int32, (BLOCK, BLOCK), 1)
    return columns <= rows


def in_vmem(n):
    return [pl.BlockSpec(memory_space=pltpu.VMEM)] * n


def in_hbm(n):
    return [pl.BlockSpec(memory_space=pltpu.HBM)] * n


def f32(*shape):
    return jax.ShapeDtypeStruct(shape, F32)


def bf16(*shape):
    return jax.ShapeDtypeStruct(shape, BF16)


def call(kernel, args, outs, name, scratch=(), in_specs=None, limit=VMEM_LIMIT):
    return pl.pallas_call(
        kernel,
        in_specs=in_specs or in_vmem(len(args)),
        out_specs=in_vmem(len(outs)),
        out_shape=outs,
        scratch_shapes=list(scratch),
        compiler_params=pltpu.CompilerParams(vmem_limit_bytes=limit),
        name=name,
    )(*args)


def scatter_rows(state_ref, send_ref, first):
    for t in range(32):
        send_ref[t, first : first + 12, :] = state_ref[12 * t : 12 * t + 12, :]


def gather_rows(got_ref, state_ref):
    for t in range(32):
        state_ref[12 * t : 12 * t + 12, :] = got_ref[t, 0:12, :]


def narrow(rows_ref, send_ref):
    for t in range(32):
        for i in range(9):
            send_ref[t, i] = rows_ref[t, 2 * i : 2 * i + 2, :]


def widen(got_ref, rows_ref):
    for t in range(32):
        for i in range(9):
            rows_ref[t, 2 * i : 2 * i + 2, :] = got_ref[t, i]


ROWS = pltpu.VMEM((32, 24, 128), F32)
STATE = pltpu.VMEM((384, 128), F32)


def time_index():
    return lax.axis_index("z") * 4 + lax.axis_index("x")


def keys_kernel(
    x_hbm, dy_hbm, w_hbm, k_ref, v_ref, out_ref, xdy_ref, x_ref, dy_ref, w_ref, sum_ref, state_ref, send_ref, frame_sem, weight_sem
):
    x_copy = pltpu.make_async_copy(x_hbm, x_ref, frame_sem.at[0])
    dy_copy = pltpu.make_async_copy(dy_hbm, dy_ref, frame_sem.at[1])
    x_copy.start()
    copies = []
    for i in range(4):
        rows = pl.ds(256 * i, 256)
        source = w_hbm.at[rows, pl.ds(INNER, 2 * INNER)]
        copies.append(pltpu.make_async_copy(source, w_ref.at[rows], weight_sem.at[i]))
        copies[-1].start()
    dy_copy.start()
    x_copy.wait()
    x = x_ref[...]
    xdy_ref[0] = x.astype(F32)
    for i in range(4):
        rows = slice(256 * i, 256 * i + 256)
        copies[i].wait()
        part = mm(x[:, rows], w_ref[rows, :])
        sum_ref[...] = part if i == 0 else sum_ref[...] + part
    norms = []
    for p in range(PAIRS):
        lanes = slice(128 * p, 128 * p + 128)
        k = sum_ref[:, lanes].astype(BF16)
        v = sum_ref[:, slice(INNER + 128 * p, INNER + 128 * p + 128)].astype(BF16)
        k_ref[:, lanes] = k
        v_ref[:, lanes] = v
        fk = features(k.astype(F32)).astype(BF16)
        state = diagonal_blocks(mm_at(fk, v))
        state_ref[64 * p : 64 * p + 64, :] = state
        norms.append(jnp.sum(fk.astype(F32), axis=0, keepdims=True))
    scatter_rows(state_ref, send_ref, 0)
    norm = jnp.concatenate(norms + [jnp.zeros((6, 128), F32)], axis=0)
    for t in range(32):
        send_ref[t, 12:24, :] = norm
    narrow(send_ref, out_ref)
    dy_copy.wait()
    xdy_ref[1] = dy_ref[...].astype(F32)


def keys(x, dy, w_qkv):
    rows, width = x.shape
    scratch = [pltpu.VMEM((rows, width), BF16)] * 2 + [pltpu.VMEM((width, 2 * INNER), BF16)]
    scratch += [pltpu.VMEM((rows, 2 * INNER), F32), STATE, ROWS]
    scratch += [pltpu.SemaphoreType.DMA((2,)), pltpu.SemaphoreType.DMA((4,))]
    outs = [bf16(rows, INNER)] * 2 + [f32(32, 9, 2, 128), f32(2, rows, width)]
    return call(keys_kernel, (x, dy, w_qkv), outs, "keys", scratch, in_hbm(3), KEYS_VMEM)


def queries_kernel(
    x_hbm, dy_hbm, w_hbm, wo_hbm, k_ref, q_ref, g_ref, w_ref, sums_ref,
    x_ref, dy_ref, wq_ref, wo_ref, sems,
):
    copies = [
        pltpu.make_async_copy(x_hbm, x_ref, sems.at[0]),
        pltpu.make_async_copy(w_hbm.at[:, pl.ds(0, INNER)], wq_ref, sems.at[1]),
        pltpu.make_async_copy(dy_hbm, dy_ref, sems.at[2]),
        pltpu.make_async_copy(wo_hbm, wo_ref, sems.at[3]),
    ]
    for copy in copies:
        copy.start()
    copies[0].wait()
    copies[1].wait()
    mask = causal()
    lane = lax.broadcasted_iota(jnp.int32, (BLOCK, 128), 1)
    packed = jnp.zeros((BLOCK, 128), F32)
    for step in range(3):
        wide = slice(256 * step, 256 * step + 256)
        q_ref[:, wide] = mm(x_ref[...], wq_ref[:, wide]).astype(BF16)
        for p in (2 * step, 2 * step + 1):
            lanes = slice(128 * p, 128 * p + 128)
            fq = features(q_ref[:, lanes].astype(F32)).astype(BF16)
            fk = features(k_ref[:, lanes].astype(F32)).astype(BF16)
            for half, rows in enumerate(split_pair(fq)):
                scores = jnp.where(mask, mm_bt(rows, fk), 0.0)
                w_ref[p, :, 128 * half : 128 * half + 128] = scores.astype(BF16)
                packed = jnp.where(lane == 2 * p + half, jnp.sum(scores, axis=1, keepdims=True), packed)
    sums_ref[...] = packed
    copies[2].wait()
    copies[3].wait()
    for step in range(3):
        wide = slice(256 * step, 256 * step + 256)
        g_ref[:, wide] = mm(dy_ref[...], wo_ref[:, wide]).astype(BF16)


def queries(x, dy, w_qkv, w_out, k):
    rows, width = x.shape
    scratch = [pltpu.VMEM((rows, width), BF16)] * 2 + [pltpu.VMEM((width, INNER), BF16)] * 2
    scratch += [pltpu.SemaphoreType.DMA((4,))]
    outs = [bf16(rows, INNER)] * 2 + [bf16(PAIRS, BLOCK, 256), f32(BLOCK, 128)]
    specs = in_hbm(4) + in_vmem(1)
    return call(queries_kernel, (x, dy, w_qkv, w_out, k), outs, "queries", scratch, specs, LARGE_VMEM)


def denominators_kernel(in_ref, q_ref, g_ref, sums_ref, send_ref, inverse_ref, dnum_ref, norm_ref, state_ref, got_ref):
    widen(in_ref, got_ref)
    me = time_index()
    carry = jnp.zeros((12, 128), F32)
    norms = jnp.zeros((6, 128), F32)
    for t in range(32):
        send_ref[t, 0:12, :] = carry
        carry = carry + got_ref[t, 0:12, :]
        norms = norms + jnp.where(t < me, got_ref[t, 12:18, :], 0.0)
    norm_ref[...] = jnp.concatenate([norms, jnp.zeros((2, 128), F32)], axis=0)
    lane = lax.broadcasted_iota(jnp.int32, (BLOCK, 128), 1)
    packed = jnp.ones((BLOCK, 128), F32)
    for p in range(PAIRS):
        lanes = slice(128 * p, 128 * p + 128)
        fq = features(q_ref[:, lanes].astype(F32)).astype(BF16)
        dots = [
            jnp.sum(a, axis=1, keepdims=True) + sums_ref[:, 2 * p + half : 2 * p + half + 1]
            for half, a in enumerate(split_pair(fq.astype(F32) * norms[p : p + 1, :]))
        ]
        for half in range(2):
            packed = jnp.where(lane == 2 * p + half, dots[half], packed)
        den = jnp.where(low_lanes((BLOCK, 128)), dots[0], dots[1])
        dnum = (g_ref[:, lanes].astype(F32) / den).astype(BF16)
        dnum_ref[:, lanes] = dnum
        dstate = diagonal_blocks(mm_at(fq, dnum))
        state_ref[64 * p : 64 * p + 64, :] = dstate
    inverse_ref[...] = 1.0 / packed
    scatter_rows(state_ref, send_ref, 12)


def denominators(*args):
    outs = [f32(32, 24, 128), f32(BLOCK, 128), bf16(BLOCK, INNER), f32(8, 128)]
    return call(denominators_kernel, args, outs, "denominators", [STATE, ROWS])


def forward_kernel(
    got_ref, q_ref, k_ref, v_ref, g_ref, inverse_ref, dnum_ref, norm_ref, w_ref,
    narrow_ref, dq_ref, ds_ref, b0_ref, b1_ref, b2_ref, b3_ref, out_ref, state_ref, send_ref,
):
    gather_rows(got_ref, state_ref)
    carry = jnp.zeros((12, 128), F32)
    for t in reversed(range(32)):
        send_ref[t, 0:12, :] = carry
        carry = carry + got_ref[t, 12:24, :]
    mask = causal()
    low = low_lanes((BLOCK, 128))
    dnorms = []
    for p in range(PAIRS):
        lanes = slice(128 * p, 128 * p + 128)
        block, part = p // 3, slice(128 * (p % 3), 128 * (p % 3) + 128)
        q = q_ref[:, lanes].astype(F32)
        fq = features(q).astype(BF16)
        fk = features(k_ref[:, lanes].astype(F32)).astype(BF16)
        v = v_ref[:, lanes]
        g = g_ref[:, lanes].astype(F32)
        inverse = jnp.where(
            low, inverse_ref[:, 2 * p : 2 * p + 1], inverse_ref[:, 2 * p + 1 : 2 * p + 2]
        )
        state = block_diagonal(state_ref[64 * p : 64 * p + 64, :].astype(BF16))
        v_halves = jnp.concatenate(split_pair(v), axis=0)
        ratio = (mm(w_ref[p], v_halves) + mm(fq, state)) * inverse
        out_ref[2 + block, :, part] = ratio.astype(BF16).astype(F32)
        dnum = dnum_ref[:, lanes]
        sums = [jnp.sum(a, axis=1, keepdims=True) for a in split_pair(g * ratio)]
        dden = -jnp.where(low, sums[0], sums[1]) * inverse
        ddens = (dden[:, 0:1], dden[:, 127:128])
        dnorms.append(jnp.sum(dden * fq.astype(F32), axis=0, keepdims=True))
        ds = [
            jnp.where(mask, mm_bt(rows, v) + column, 0.0).astype(BF16)
            for rows, column in zip(split_pair(dnum), ddens)
        ]
        ds_ref[p] = jnp.concatenate(ds, axis=0)
        dfq = (
            mm(jnp.concatenate(ds, axis=1), jnp.concatenate(split_pair(fk), axis=0))
            + mm_bt(dnum, state)
            + dden * norm_ref[p : p + 1, :]
        )
        dq = (dfq * slope(q)).astype(BF16)
        dq_ref[:, lanes] = dq
        out_ref[block, :, part] = dq.astype(F32)
    dnorm = jnp.concatenate(dnorms + [jnp.zeros((6, 128), F32)], axis=0)
    for t in range(32):
        send_ref[t, 12:24, :] = dnorm
    narrow(send_ref, narrow_ref)
    y = lax.axis_index("y")
    for i, ref in enumerate((b0_ref, b1_ref, b2_ref, b3_ref)):
        ref[...] = out_ref[lax.rem(y + i, 4)]


def forward(*args):
    outs = [f32(32, 9, 2, 128), bf16(BLOCK, INNER), bf16(PAIRS, 256, 128)] + [f32(BLOCK, 384)] * 4
    return call(forward_kernel, args, outs, "forward", [pltpu.VMEM((4, BLOCK, 384), F32), STATE, ROWS])


def backward_kernel(
    in_ref, q_ref, k_ref, v_ref, dnum_ref, w_ref, ds_ref, out_ref, dkv_ref, state_ref, got_ref
):
    widen(in_ref, got_ref)
    me = time_index()
    dnorms = jnp.zeros((6, 128), F32)
    for t in range(32):
        dnorms = dnorms + jnp.where(t > me, got_ref[t, 12:18, :], 0.0)
    gather_rows(got_ref, state_ref)
    for p in range(PAIRS):
        lanes = slice(128 * p, 128 * p + 128)
        block, part = p // 3, slice(128 * (p % 3), 128 * (p % 3) + 128)
        fq = features(q_ref[:, lanes].astype(F32)).astype(BF16)
        k = k_ref[:, lanes].astype(F32)
        fk = features(k).astype(BF16)
        v = v_ref[:, lanes]
        dnum = dnum_ref[:, lanes]
        dstate = block_diagonal(state_ref[64 * p : 64 * p + 64, :].astype(BF16))
        dfk = (
            mm_at(ds_ref[p], jnp.concatenate(split_pair(fq), axis=0))
            + mm_bt(v, dstate)
            + dnorms[p : p + 1, :]
        )
        dk = (dfk * slope(k)).astype(BF16)
        w = jnp.concatenate([w_ref[p, :, 0:128], w_ref[p, :, 128:256]], axis=0)
        dv = (mm_at(w, jnp.concatenate(split_pair(dnum), axis=0)) + mm(fk, dstate)).astype(BF16)
        out_ref[block, :, part] = dk.astype(F32)
        out_ref[2 + block, :, part] = dv.astype(F32)
        dkv_ref[:, lanes] = dk
        dkv_ref[:, slice(INNER + 128 * p, INNER + 128 * p + 128)] = dv


def backward(*args):
    return call(backward_kernel, args, [f32(4, BLOCK, 384), bf16(BLOCK, 2 * INNER)], "backward", [STATE, ROWS])


def stage_kernel(xdy_ref, x_ref, chosen_ref):
    y = lax.axis_index("y")
    sources = [lax.rem(y + 4 - i, 4) for i in range(4)]
    for j in range(8):
        lanes = slice(128 * j, 128 * j + 128)
        x = jnp.concatenate([xdy_ref[i, 0, :, lanes] for i in sources], axis=0)
        dy = jnp.concatenate([xdy_ref[i, 1, :, lanes] for i in sources], axis=0)
        x_ref[lanes, :] = x.T.astype(BF16)
        chosen_ref[lanes, :] = jnp.where(y < 2, x, dy).T.astype(BF16)


def weights_kernel(x_ref, chosen_ref, b0_ref, b1_ref, b2_ref, b3_ref, got_ref, keep_ref, give_ref):
    y, c = lax.axis_index("y"), lax.axis_index("c")
    first = [b0_ref[...], b1_ref[...], b2_ref[...], b3_ref[...]]
    second = [got_ref[lax.rem(y + s, 4)] for s in (0, 3, 2, 1)]
    for frames_ref, blocks, lanes in (
        (chosen_ref, first, slice(0, 384)),
        (x_ref, second, slice(384, 768)),
    ):
        blocks = jnp.concatenate(blocks, axis=0).astype(BF16)
        for j in range(4):
            part = mm(frames_ref[256 * j : 256 * j + 256, :], blocks).reshape(2, 4, 2, 16, 384)
            for i in range(4):
                one, two = part[:, i, 0], part[:, i, 1]
                keep_ref[i, 2 * j : 2 * j + 2, :, lanes] = jnp.where(c == 0, one, two)
                give_ref[i, 2 * j : 2 * j + 2, :, lanes] = jnp.where(c == 0, two, one)


def core_sum_kernel(keep_ref, got_ref, out_ref):
    out_ref[...] = keep_ref[...] + got_ref[...]


def row_sum_kernel(got_ref, out_ref):
    out_ref[...] = (got_ref[0] + got_ref[1]) + (got_ref[2] + got_ref[3])


def spread_kernel(got_ref, out_ref):
    total = got_ref[0]
    for i in range(1, 8):
        total = total + got_ref[i]
    for i in range(8):
        out_ref[i] = total


def frame_gradient_kernel(dq_ref, dkv_ref, w_ref, out_ref):
    for j in range(4):
        rows = slice(256 * j, 256 * j + 256)
        dx = mm_bt(dq_ref[...], w_ref[rows, 0:INNER]) + mm_bt(dkv_ref[...], w_ref[rows, INNER:])
        out_ref[:, rows] = dx.astype(BF16)


def assemble_kernel(got_ref, qkv_ref, out_ref):
    for y in range(4):
        for c in range(2):
            rows = slice(16 * c, 16 * c + 16)
            piece = got_ref[2 * y + c]
            target = qkv_ref if y < 2 else out_ref
            target[rows, 384 * (y % 2) : 384 * (y % 2) + 384] = piece[:, 0:384]
            qkv_ref[rows, INNER + 384 * y : INNER + 384 * y + 384] = piece[:, 384:768]


def swap(a, axes):
    return lax.all_to_all(a, axes, 0, 0, tiled=True)


def shift(a, axis, s):
    n = lax.axis_size(axis)
    return lax.ppermute(a, axis, [(i, (i + s) % n) for i in range(n)])


def together(*values):
    return lax.optimization_barrier(values)


def per_device(frames, grad_frames, w_qkv, w_out):
    k, v, send, xdy = keys(frames[0], grad_frames[0], w_qkv)
    xdy = lax.all_gather(xdy, "y")
    q, g, w, sums = queries(frames[0], grad_frames[0], w_qkv, w_out, k)
    got, q, g, w, sums = together(swap(send, TM), q, g, w, sums)
    send, inverse, dnum, norm = denominators(got, q, g, sums)
    send, dq, ds, *first = forward(swap(send, TM), q, k, v, g, inverse, dnum, norm, w)
    first = [first[0]] + [shift(a, "y", s) for s, a in enumerate(first) if s]
    x, chosen = call(stage_kernel, (xdy,), [bf16(1024, 512)] * 2, "stage", limit=LARGE_VMEM)
    got, first, x, chosen = together(swap(send, TM), first, x, chosen)
    second, dkv = backward(got, q, k, v, dnum, w, ds)
    second = swap(second, "y")
    out = [f32(4, 8, 16, 768)] * 2
    keep, give = call(weights_kernel, (x, chosen, *first, second), out, "weights")
    (part,) = call(core_sum_kernel, (keep, shift(give, "c", 1)), out[:1], "core_sum")
    (part,) = call(row_sum_kernel, (swap(part, "x"),), [f32(8, 16, 768)], "row_sum")
    (part,) = call(spread_kernel, (swap(part, "z"),), [f32(8, 16, 768)], "spread")
    part = swap(part, DP)
    (dx,) = call(frame_gradient_kernel, (dq, dkv, w_qkv), [bf16(BLOCK, 1024)], "frame_gradient", limit=LARGE_VMEM)
    grad_qkv, grad_out = call(assemble_kernel, (part,), [f32(32, 3 * INNER), f32(32, INNER)], "assemble")
    return dx[None], grad_qkv, grad_out


def solution(mesh):
    torus = Mesh(mesh.devices.reshape(8, 4, 4, 2), TM + DP)
    rows = P(DP, TM, None)
    return jax.shard_map(
        per_device,
        mesh=torus,
        in_specs=(rows, rows, P(), P()),
        out_specs=(rows, P(TM, None), P(TM, None)),
        check_vma=False,
    )
```

```python
import jax
import jax.numpy as jnp
from jax import lax
from jax.experimental import pallas as pl
from jax.experimental.pallas import tpu as pltpu
from jax.sharding import Mesh
from jax.sharding import PartitionSpec as P

HEADS = 12
HEAD = 64
BLOCK = 128
PAIRS = HEADS // 2
INNER = HEADS * HEAD
TM = ("z", "x")
DP = ("y", "c")
F32 = jnp.float32
BF16 = jnp.bfloat16
VMEM_LIMIT = 32 * 1024 * 1024
LARGE_VMEM = 54300 * 1024
KEYS_VMEM = 54600 * 1024


def features(a):
    return jnp.where(a > 0, a + 1.0, jnp.exp(jnp.minimum(a, 0.0)))


def slope(a):
    return jnp.where(a > 0, 1.0, jnp.exp(jnp.minimum(a, 0.0)))


def low_lanes(shape):
    return lax.broadcasted_iota(jnp.int32, shape, len(shape) - 1) < HEAD


def split_pair(a):
    low = low_lanes(a.shape)
    zero = jnp.zeros_like(a)
    return jnp.where(low, a, zero), jnp.where(low, zero, a)


def block_diagonal(packed):
    first, second = split_pair(packed)
    return jnp.concatenate([first, second], axis=0)


def diagonal_blocks(m):
    return jnp.where(low_lanes((HEAD, 2 * HEAD)), m[:HEAD], m[HEAD:])


def mm(a, b):
    return lax.dot_general(a, b, (((1,), (0,)), ((), ())), preferred_element_type=F32)


def mm_bt(a, b):
    return lax.dot_general(a, b, (((1,), (1,)), ((), ())), preferred_element_type=F32)


def mm_at(a, b):
    return lax.dot_general(a, b, (((0,), (0,)), ((), ())), preferred_element_type=F32)


def causal():
    rows = lax.broadcasted_iota(jnp.int32, (BLOCK, BLOCK), 0)
    columns = lax.broadcasted_iota(jnp.int32, (BLOCK, BLOCK), 1)
    return columns <= rows


def in_vmem(n):
    return [pl.BlockSpec(memory_space=pltpu.VMEM)] * n


def in_hbm(n):
    return [pl.BlockSpec(memory_space=pltpu.HBM)] * n


def f32(*shape):
    return jax.ShapeDtypeStruct(shape, F32)


def bf16(*shape):
    return jax.ShapeDtypeStruct(shape, BF16)


def call(kernel, args, outs, name, scratch=(), in_specs=None, limit=VMEM_LIMIT):
    return pl.pallas_call(
        kernel,
        in_specs=in_specs or in_vmem(len(args)),
        out_specs=in_vmem(len(outs)),
        out_shape=outs,
        scratch_shapes=list(scratch),
        compiler_params=pltpu.CompilerParams(vmem_limit_bytes=limit),
        name=name,
    )(*args)


def scatter_rows(state_ref, send_ref, first):
    for t in range(32):
        send_ref[t, first : first + 12, :] = state_ref[12 * t : 12 * t + 12, :]


def gather_rows(got_ref, state_ref):
    for t in range(32):
        state_ref[12 * t : 12 * t + 12, :] = got_ref[t, 0:12, :]


def narrow(rows_ref, send_ref):
    for t in range(32):
        for i in range(9):
            send_ref[t, i] = rows_ref[t, 2 * i : 2 * i + 2, :]


def widen(got_ref, rows_ref):
    for t in range(32):
        for i in range(9):
            rows_ref[t, 2 * i : 2 * i + 2, :] = got_ref[t, i]


ROWS = pltpu.VMEM((32, 24, 128), F32)
STATE = pltpu.VMEM((384, 128), F32)


def time_index():
    return lax.axis_index("z") * 4 + lax.axis_index("x")


def keys_kernel(
    x_hbm, dy_hbm, w_hbm, k_ref, v_ref, out_ref, xdy_ref, x_ref, dy_ref, w_ref, sum_ref, state_ref, send_ref, frame_sem, weight_sem
):
    x_copy = pltpu.make_async_copy(x_hbm, x_ref, frame_sem.at[0])
    dy_copy = pltpu.make_async_copy(dy_hbm, dy_ref, frame_sem.at[1])
    x_copy.start()
    copies = []
    for i in range(4):
        rows = pl.ds(256 * i, 256)
        source = w_hbm.at[rows, pl.ds(INNER, 2 * INNER)]
        copies.append(pltpu.make_async_copy(source, w_ref.at[rows], weight_sem.at[i]))
        copies[-1].start()
    dy_copy.start()
    x_copy.wait()
    x = x_ref[...]
    xdy_ref[0] = x.astype(F32)
    for i in range(4):
        rows = slice(256 * i, 256 * i + 256)
        copies[i].wait()
        part = mm(x[:, rows], w_ref[rows, :])
        sum_ref[...] = part if i == 0 else sum_ref[...] + part
    norms = []
    for p in range(PAIRS):
        lanes = slice(128 * p, 128 * p + 128)
        k = sum_ref[:, lanes].astype(BF16)
        v = sum_ref[:, slice(INNER + 128 * p, INNER + 128 * p + 128)].astype(BF16)
        k_ref[:, lanes] = k
        v_ref[:, lanes] = v
        fk = features(k.astype(F32)).astype(BF16)
        state = diagonal_blocks(mm_at(fk, v))
        state_ref[64 * p : 64 * p + 64, :] = state
        norms.append(jnp.sum(fk.astype(F32), axis=0, keepdims=True))
    scatter_rows(state_ref, send_ref, 0)
    norm = jnp.concatenate(norms + [jnp.zeros((6, 128), F32)], axis=0)
    for t in range(32):
        send_ref[t, 12:24, :] = norm
    narrow(send_ref, out_ref)
    dy_copy.wait()
    xdy_ref[1] = dy_ref[...].astype(F32)


def keys(x, dy, w_qkv):
    rows, width = x.shape
    scratch = [pltpu.VMEM((rows, width), BF16)] * 2 + [pltpu.VMEM((width, 2 * INNER), BF16)]
    scratch += [pltpu.VMEM((rows, 2 * INNER), F32), STATE, ROWS]
    scratch += [pltpu.SemaphoreType.DMA((2,)), pltpu.SemaphoreType.DMA((4,))]
    outs = [bf16(rows, INNER)] * 2 + [f32(32, 9, 2, 128), f32(2, rows, width)]
    return call(keys_kernel, (x, dy, w_qkv), outs, "keys", scratch, in_hbm(3), KEYS_VMEM)


def queries_kernel(
    x_hbm, dy_hbm, w_hbm, wo_hbm, k_ref, q_ref, g_ref, w_ref, sums_ref,
    x_ref, dy_ref, wq_ref, wo_ref, sems,
):
    copies = [
        pltpu.make_async_copy(x_hbm, x_ref, sems.at[0]),
        pltpu.make_async_copy(w_hbm.at[:, pl.ds(0, INNER)], wq_ref, sems.at[1]),
        pltpu.make_async_copy(dy_hbm, dy_ref, sems.at[2]),
        pltpu.make_async_copy(wo_hbm, wo_ref, sems.at[3]),
    ]
    for copy in copies:
        copy.start()
    copies[0].wait()
    copies[1].wait()
    mask = causal()
    lane = lax.broadcasted_iota(jnp.int32, (BLOCK, 128), 1)
    packed = jnp.zeros((BLOCK, 128), F32)
    for step in range(3):
        wide = slice(256 * step, 256 * step + 256)
        q_ref[:, wide] = mm(x_ref[...], wq_ref[:, wide]).astype(BF16)
        for p in (2 * step, 2 * step + 1):
            lanes = slice(128 * p, 128 * p + 128)
            fq = features(q_ref[:, lanes].astype(F32)).astype(BF16)
            fk = features(k_ref[:, lanes].astype(F32)).astype(BF16)
            for half, rows in enumerate(split_pair(fq)):
                scores = jnp.where(mask, mm_bt(rows, fk), 0.0)
                w_ref[p, :, 128 * half : 128 * half + 128] = scores.astype(BF16)
                packed = jnp.where(lane == 2 * p + half, jnp.sum(scores, axis=1, keepdims=True), packed)
    sums_ref[...] = packed
    copies[2].wait()
    copies[3].wait()
    for step in range(3):
        wide = slice(256 * step, 256 * step + 256)
        g_ref[:, wide] = mm(dy_ref[...], wo_ref[:, wide]).astype(BF16)


def queries(x, dy, w_qkv, w_out, k):
    rows, width = x.shape
    scratch = [pltpu.VMEM((rows, width), BF16)] * 2 + [pltpu.VMEM((width, INNER), BF16)] * 2
    scratch += [pltpu.SemaphoreType.DMA((4,))]
    outs = [bf16(rows, INNER)] * 2 + [bf16(PAIRS, BLOCK, 256), f32(BLOCK, 128)]
    specs = in_hbm(4) + in_vmem(1)
    return call(queries_kernel, (x, dy, w_qkv, w_out, k), outs, "queries", scratch, specs, LARGE_VMEM)


def denominators_kernel(in_ref, q_ref, g_ref, sums_ref, send_ref, inverse_ref, dnum_ref, norm_ref, state_ref, got_ref):
    widen(in_ref, got_ref)
    me = time_index()
    carry = jnp.zeros((12, 128), F32)
    norms = jnp.zeros((6, 128), F32)
    for t in range(32):
        send_ref[t, 0:12, :] = carry
        carry = carry + got_ref[t, 0:12, :]
        norms = norms + jnp.where(t < me, got_ref[t, 12:18, :], 0.0)
    norm_ref[...] = jnp.concatenate([norms, jnp.zeros((2, 128), F32)], axis=0)
    lane = lax.broadcasted_iota(jnp.int32, (BLOCK, 128), 1)
    packed = jnp.ones((BLOCK, 128), F32)
    for p in range(PAIRS):
        lanes = slice(128 * p, 128 * p + 128)
        fq = features(q_ref[:, lanes].astype(F32)).astype(BF16)
        dots = [
            jnp.sum(a, axis=1, keepdims=True) + sums_ref[:, 2 * p + half : 2 * p + half + 1]
            for half, a in enumerate(split_pair(fq.astype(F32) * norms[p : p + 1, :]))
        ]
        for half in range(2):
            packed = jnp.where(lane == 2 * p + half, dots[half], packed)
        den = jnp.where(low_lanes((BLOCK, 128)), dots[0], dots[1])
        dnum = (g_ref[:, lanes].astype(F32) / den).astype(BF16)
        dnum_ref[:, lanes] = dnum
        dstate = diagonal_blocks(mm_at(fq, dnum))
        state_ref[64 * p : 64 * p + 64, :] = dstate
    inverse_ref[...] = 1.0 / packed
    scatter_rows(state_ref, send_ref, 12)


def denominators(*args):
    outs = [f32(32, 24, 128), f32(BLOCK, 128), bf16(BLOCK, INNER), f32(8, 128)]
    return call(denominators_kernel, args, outs, "denominators", [STATE, ROWS])


def forward_kernel(
    got_ref, q_ref, k_ref, v_ref, g_ref, inverse_ref, dnum_ref, norm_ref, w_ref,
    narrow_ref, dq_ref, ds_ref, b0_ref, b1_ref, b2_ref, b3_ref, out_ref, state_ref, send_ref,
):
    gather_rows(got_ref, state_ref)
    carry = jnp.zeros((12, 128), F32)
    for t in reversed(range(32)):
        send_ref[t, 0:12, :] = carry
        carry = carry + got_ref[t, 12:24, :]
    mask = causal()
    low = low_lanes((BLOCK, 128))
    dnorms = []
    for p in range(PAIRS):
        lanes = slice(128 * p, 128 * p + 128)
        block, part = p // 3, slice(128 * (p % 3), 128 * (p % 3) + 128)
        q = q_ref[:, lanes].astype(F32)
        fq = features(q).astype(BF16)
        fk = features(k_ref[:, lanes].astype(F32)).astype(BF16)
        v = v_ref[:, lanes]
        g = g_ref[:, lanes].astype(F32)
        inverse = jnp.where(
            low, inverse_ref[:, 2 * p : 2 * p + 1], inverse_ref[:, 2 * p + 1 : 2 * p + 2]
        )
        state = block_diagonal(state_ref[64 * p : 64 * p + 64, :].astype(BF16))
        v_halves = jnp.concatenate(split_pair(v), axis=0)
        ratio = (mm(w_ref[p], v_halves) + mm(fq, state)) * inverse
        out_ref[2 + block, :, part] = ratio.astype(BF16).astype(F32)
        dnum = dnum_ref[:, lanes]
        sums = [jnp.sum(a, axis=1, keepdims=True) for a in split_pair(g * ratio)]
        dden = -jnp.where(low, sums[0], sums[1]) * inverse
        ddens = (dden[:, 0:1], dden[:, 127:128])
        dnorms.append(jnp.sum(dden * fq.astype(F32), axis=0, keepdims=True))
        ds = [
            jnp.where(mask, mm_bt(rows, v) + column, 0.0).astype(BF16)
            for rows, column in zip(split_pair(dnum), ddens)
        ]
        ds_ref[p] = jnp.concatenate(ds, axis=0)
        dfq = (
            mm(jnp.concatenate(ds, axis=1), jnp.concatenate(split_pair(fk), axis=0))
            + mm_bt(dnum, state)
            + dden * norm_ref[p : p + 1, :]
        )
        dq = (dfq * slope(q)).astype(BF16)
        dq_ref[:, lanes] = dq
        out_ref[block, :, part] = dq.astype(F32)
    dnorm = jnp.concatenate(dnorms + [jnp.zeros((6, 128), F32)], axis=0)
    for t in range(32):
        send_ref[t, 12:24, :] = dnorm
    narrow(send_ref, narrow_ref)
    y = lax.axis_index("y")
    for i, ref in enumerate((b0_ref, b1_ref, b2_ref, b3_ref)):
        ref[...] = out_ref[lax.rem(y + i, 4)]


def forward(*args):
    outs = [f32(32, 9, 2, 128), bf16(BLOCK, INNER), bf16(PAIRS, 256, 128)] + [f32(BLOCK, 384)] * 4
    return call(forward_kernel, args, outs, "forward", [pltpu.VMEM((4, BLOCK, 384), F32), STATE, ROWS])


def backward_kernel(
    in_ref, q_ref, k_ref, v_ref, dnum_ref, w_ref, ds_ref, out_ref, dkv_ref, state_ref, got_ref
):
    widen(in_ref, got_ref)
    me = time_index()
    dnorms = jnp.zeros((6, 128), F32)
    for t in range(32):
        dnorms = dnorms + jnp.where(t > me, got_ref[t, 12:18, :], 0.0)
    gather_rows(got_ref, state_ref)
    for p in range(PAIRS):
        lanes = slice(128 * p, 128 * p + 128)
        block, part = p // 3, slice(128 * (p % 3), 128 * (p % 3) + 128)
        fq = features(q_ref[:, lanes].astype(F32)).astype(BF16)
        k = k_ref[:, lanes].astype(F32)
        fk = features(k).astype(BF16)
        v = v_ref[:, lanes]
        dnum = dnum_ref[:, lanes]
        dstate = block_diagonal(state_ref[64 * p : 64 * p + 64, :].astype(BF16))
        dfk = (
            mm_at(ds_ref[p], jnp.concatenate(split_pair(fq), axis=0))
            + mm_bt(v, dstate)
            + dnorms[p : p + 1, :]
        )
        dk = (dfk * slope(k)).astype(BF16)
        w = jnp.concatenate([w_ref[p, :, 0:128], w_ref[p, :, 128:256]], axis=0)
        dv = (mm_at(w, jnp.concatenate(split_pair(dnum), axis=0)) + mm(fk, dstate)).astype(BF16)
        out_ref[block, :, part] = dk.astype(F32)
        out_ref[2 + block, :, part] = dv.astype(F32)
        dkv_ref[:, lanes] = dk
        dkv_ref[:, slice(INNER + 128 * p, INNER + 128 * p + 128)] = dv


def backward(*args):
    return call(backward_kernel, args, [f32(4, BLOCK, 384), bf16(BLOCK, 2 * INNER)], "backward", [STATE, ROWS])


def stage_kernel(xdy_ref, x_ref, chosen_ref):
    y = lax.axis_index("y")
    sources = [lax.rem(y + 4 - i, 4) for i in range(4)]
    for j in range(8):
        lanes = slice(128 * j, 128 * j + 128)
        x = jnp.concatenate([xdy_ref[i, 0, :, lanes] for i in sources], axis=0)
        dy = jnp.concatenate([xdy_ref[i, 1, :, lanes] for i in sources], axis=0)
        x_ref[lanes, :] = x.T.astype(BF16)
        chosen_ref[lanes, :] = jnp.where(y < 2, x, dy).T.astype(BF16)


def weights_kernel(x_ref, chosen_ref, b0_ref, b1_ref, b2_ref, b3_ref, got_ref, keep_ref, give_ref):
    y, c = lax.axis_index("y"), lax.axis_index("c")
    first = [b0_ref[...], b1_ref[...], b2_ref[...], b3_ref[...]]
    second = [got_ref[lax.rem(y + s, 4)] for s in (0, 3, 2, 1)]
    for frames_ref, blocks, lanes in (
        (chosen_ref, first, slice(0, 384)),
        (x_ref, second, slice(384, 768)),
    ):
        blocks = jnp.concatenate(blocks, axis=0).astype(BF16)
        for j in range(4):
            part = mm(frames_ref[256 * j : 256 * j + 256, :], blocks).reshape(2, 4, 2, 16, 384)
            for i in range(4):
                one, two = part[:, i, 0], part[:, i, 1]
                keep_ref[i, 2 * j : 2 * j + 2, :, lanes] = jnp.where(c == 0, one, two)
                give_ref[i, 2 * j : 2 * j + 2, :, lanes] = jnp.where(c == 0, two, one)


def core_sum_kernel(keep_ref, got_ref, out_ref):
    out_ref[...] = keep_ref[...] + got_ref[...]


def row_sum_kernel(got_ref, out_ref):
    out_ref[...] = (got_ref[0] + got_ref[1]) + (got_ref[2] + got_ref[3])


def spread_kernel(got_ref, out_ref):
    total = got_ref[0]
    for i in range(1, 8):
        total = total + got_ref[i]
    for i in range(8):
        out_ref[i] = total


def frame_gradient_kernel(dq_ref, dkv_ref, w_ref, out_ref):
    for j in range(4):
        rows = slice(256 * j, 256 * j + 256)
        dx = mm_bt(dq_ref[...], w_ref[rows, 0:INNER]) + mm_bt(dkv_ref[...], w_ref[rows, INNER:])
        out_ref[:, rows] = dx.astype(BF16)


def assemble_kernel(got_ref, qkv_ref, out_ref):
    for y in range(4):
        for c in range(2):
            rows = slice(16 * c, 16 * c + 16)
            piece = got_ref[2 * y + c]
            target = qkv_ref if y < 2 else out_ref
            target[rows, 384 * (y % 2) : 384 * (y % 2) + 384] = piece[:, 0:384]
            qkv_ref[rows, INNER + 384 * y : INNER + 384 * y + 384] = piece[:, 384:768]


def swap(a, axes):
    return lax.all_to_all(a, axes, 0, 0, tiled=True)


def shift(a, axis, s):
    n = lax.axis_size(axis)
    return lax.ppermute(a, axis, [(i, (i + s) % n) for i in range(n)])


def together(*values):
    return lax.optimization_barrier(values)


def per_device(frames, grad_frames, w_qkv, w_out):
    k, v, send, xdy = keys(frames[0], grad_frames[0], w_qkv)
    xdy = lax.all_gather(xdy, "y")
    q, g, w, sums = queries(frames[0], grad_frames[0], w_qkv, w_out, k)
    got, q, g, w, sums = together(swap(send, TM), q, g, w, sums)
    send, inverse, dnum, norm = denominators(got, q, g, sums)
    send, dq, ds, *first = forward(swap(send, TM), q, k, v, g, inverse, dnum, norm, w)
    first = [first[0]] + [shift(a, "y", s) for s, a in enumerate(first) if s]
    x, chosen = call(stage_kernel, (xdy,), [bf16(1024, 512)] * 2, "stage", limit=LARGE_VMEM)
    got, first, x, chosen = together(swap(send, TM), first, x, chosen)
    second, dkv = backward(got, q, k, v, dnum, w, ds)
    second = swap(second, "y")
    out = [f32(4, 8, 16, 768)] * 2
    keep, give = call(weights_kernel, (x, chosen, *first, second), out, "weights")
    (part,) = call(core_sum_kernel, (keep, shift(give, "c", 1)), out[:1], "core_sum")
    (part,) = call(row_sum_kernel, (swap(part, "x"),), [f32(8, 16, 768)], "row_sum")
    (dx,) = call(frame_gradient_kernel, (dq, dkv, w_qkv), [bf16(BLOCK, 1024)], "frame_gradient", limit=LARGE_VMEM)
    part, dx = together(swap(part, "z"), dx)
    (part,) = call(spread_kernel, (part,), [f32(8, 16, 768)], "spread")
    part = swap(part, DP)
    grad_qkv, grad_out = call(assemble_kernel, (part,), [f32(32, 3 * INNER), f32(32, INNER)], "assemble")
    return dx[None], grad_qkv, grad_out


def solution(mesh):
    torus = Mesh(mesh.devices.reshape(8, 4, 4, 2), TM + DP)
    rows = P(DP, TM, None)
    return jax.shard_map(
        per_device,
        mesh=torus,
        in_specs=(rows, rows, P(), P()),
        out_specs=(rows, P(TM, None), P(TM, None)),
        check_vma=False,
    )
```
